32 devices in a mesh: tm: 8 (over y, x, core), space: 4 (over z).
Axes of the slice: x: 2, y: 2, z: 4, core: 2. Of those that a mesh axis runs over, the one named last changes fastest.
Arguments:
- initial_state: float32 [64, 512], P(None, 'space'), may hold values from -6 to 6
- forcing: float32 [32, 64, 512], P('tm', None, 'space'), may hold values from -4 to 4
- coarse_gain: float32 [8, 64, 512], P('tm', None, 'space'), may hold values from 0.05 to 1, as said below
- block_inverse: float32 [64, 64, 512], P(None, None, 'space'), may hold values from -0.25 to 1.1
- face_blocks: float32 [6, 64, 64], replicated, may hold values from -0.1875 to 0.1875
- neighbor: int32 [6, 512], P(None, 'space'), may hold values from -1 to 255, as said below
- send_rows: int32 [2, 256], P(None, 'space'), may hold values from 0 to 127, as said below
Outputs:
- coarse_end: float32 [8, 64, 512], P('tm', None, 'space')
- residual: float32 [8, 64, 512], P('tm', None, 'space')
The draws below stay inside these ranges and needn't reach their ends.
Inputs may be any that keep to these rules, and one draw needn't show every extreme that they name: `neighbor`: for face f (-x, +x, -y, +y, -z, +z) of the element in local column e, the local column of its neighbour in the extended field of its partition; -1 where the face lies on the domain's side along x or y. `send_rows`: row 0 lists the local columns of a partition's lowest element layer, row 1 those of its highest, in the same order of x and y. `coarse_gain`: Positive, below one.
All inputs are finite; a program needn't handle non-finite values.
Results may differ from the reference program's by a relative error of at most 0.00014.
Values sent between devices are 32-bit elements; how exact they have to be, the bound alone decides.
A program may use at most 64 MiB of HBM per device.

```python
import jax
import jax.numpy as jnp
from jax import lax

BLOCK_VALUES = 64
GX = 8
GY = 8
STEPS = 4
SWEEPS = 2
ITERS = 2
E_DEV = 128
ELEMENT_TOTAL = 512
TIME_SLICES = 8
NF = 32
N_SPACE = 4


def grid_slots(key):
    random_key_array = jax.random.split(key, N_SPACE)
    return jax.vmap(lambda part_key: jax.random.permutation(part_key, E_DEV))(random_key_array).astype(jnp.int32)


def draw_neighbor(key, part):
    slot_table = grid_slots(key)
    layer_size = GX * GY
    grid_cell = jnp.argsort(slot_table, axis=1, stable=True).astype(jnp.int32)
    z_level = grid_cell // layer_size
    within = grid_cell % layer_size
    y_index = within // GX
    x_index = within % GX

    def lookup(target):
        return jnp.take_along_axis(slot_table, jnp.clip(target, 0, E_DEV - 1), axis=1)
    minus_x = jnp.where(x_index > 0, lookup(grid_cell - 1), -1)
    plus_x = jnp.where(x_index < GX - 1, lookup(grid_cell + 1), -1)
    minus_y = jnp.where(y_index > 0, lookup(grid_cell - GX), -1)
    plus_y = jnp.where(y_index < GY - 1, lookup(grid_cell + GX), -1)
    minus_z = jnp.where(z_level > 0, lookup(grid_cell - layer_size), E_DEV + within)
    plus_z = jnp.where(z_level < 1, lookup(grid_cell + layer_size), E_DEV + layer_size + within)
    stacked = jnp.stack([minus_x, plus_x, minus_y, plus_y, minus_z, plus_z], axis=0)
    return stacked.reshape(6, N_SPACE * E_DEV).astype(jnp.int32)


def draw_send_rows(key, part):
    slot_table = grid_slots(key)
    layer_size = GX * GY
    stacked = jnp.stack([slot_table[:, :layer_size], slot_table[:, layer_size:]], axis=0)
    return stacked.reshape(2, N_SPACE * layer_size).astype(jnp.int32)


def draw_block_inverse(key, part):
    key = jax.random.fold_in(key, 3)
    random_key_array = jax.random.split(key, 2)
    shape_full = (BLOCK_VALUES, BLOCK_VALUES, ELEMENT_TOTAL)
    elem_scale = jnp.exp(jax.random.uniform(random_key_array[0], (1, 1, ELEMENT_TOTAL), minval=jnp.log(0.5), maxval=jnp.log(0.9)))
    noise_part = jnp.clip(jax.random.normal(random_key_array[1], shape_full), -4.0, 4.0)
    row_index = lax_iota(BLOCK_VALUES)[:, None, None]
    col_index = lax_iota(BLOCK_VALUES)[None, :, None]
    identity = (row_index == col_index).astype(jnp.float32)
    return (elem_scale * (identity + 0.05 * noise_part)).astype(jnp.float32)


def lax_iota(count):
    return jnp.arange(count, dtype=jnp.int32)


def draw_coarse_gain(key, part):
    key = jax.random.fold_in(key, 5)
    random_key_array = jax.random.split(key, 4)
    rate_low = 0.1 / TIME_SLICES
    rate_high = 1.5
    damping_rate = jnp.exp(jax.random.uniform(random_key_array[0], (1, BLOCK_VALUES, ELEMENT_TOTAL), minval=jnp.log(rate_low), maxval=jnp.log(rate_high)))
    random_perturbation = jax.random.uniform(random_key_array[1], (TIME_SLICES, BLOCK_VALUES, ELEMENT_TOTAL), minval=0.5, maxval=1.5)
    spike_event = jax.random.uniform(random_key_array[2], (TIME_SLICES, BLOCK_VALUES, ELEMENT_TOTAL)) < 2.0 / TIME_SLICES
    spike_depth = jax.random.uniform(random_key_array[3], (TIME_SLICES, BLOCK_VALUES, ELEMENT_TOTAL), minval=0.5, maxval=0.8)
    gain_factors = jnp.exp(-damping_rate * random_perturbation) * jnp.where(spike_event, spike_depth, 1.0)
    return gain_factors.astype(jnp.float32)


def shard_levels(own_key, extent, pieces, smallest, top_value):
    factor_of = 1.0
    for axis_at, blocks in pieces:
        steps = jax.random.uniform(jax.random.fold_in(jax.random.fold_in(own_key, 6), axis_at), (blocks,), jnp.float32, smallest / len(pieces), top_value / len(pieces))
        factor_of = factor_of * jnp.repeat(jnp.exp(steps), extent[axis_at] // blocks).reshape((-1,) + (1,) * (len(extent) - 1 - axis_at))
    return factor_of


def bell_draw(stream_key, extent, width, reach, pieces=(), kind=jnp.bfloat16):
    drawn = jax.random.normal(stream_key, extent, jnp.float32) * width
    if len(pieces) > 0:
        drawn = shard_levels(stream_key, extent, pieces, -0.22, 0.18) * drawn
    return jnp.clip(drawn, min=-reach, max=reach).astype(kind)


def setup_inputs(seed: int = 0) -> dict:
    arg_keys = jax.random.split(jax.random.key(seed), 8)
    initial_state = bell_draw(arg_keys[0], (BLOCK_VALUES, ELEMENT_TOTAL), 1.0, 6.0, ((1, 4),), jnp.float32)
    forcing = bell_draw(arg_keys[1], (NF, BLOCK_VALUES, ELEMENT_TOTAL), 0.5, 4.0, ((0, 8), (2, 4)), jnp.float32)
    coarse_gain = draw_coarse_gain(jax.random.fold_in(arg_keys[7], 71), 0)
    block_inverse = draw_block_inverse(jax.random.fold_in(arg_keys[7], 71), 0)
    face_blocks = bell_draw(arg_keys[4], (6, BLOCK_VALUES, BLOCK_VALUES), (18 * BLOCK_VALUES) ** -0.5, 0.1875, (), jnp.float32)
    neighbor = draw_neighbor(jax.random.fold_in(arg_keys[7], 71), 0)
    send_rows = draw_send_rows(jax.random.fold_in(arg_keys[7], 71), 0)
    return {"initial_state": initial_state, "forcing": forcing, "coarse_gain": coarse_gain, "block_inverse": block_inverse, "face_blocks": face_blocks, "neighbor": neighbor, "send_rows": send_rows}


HIGHEST_PRECISION = lax.Precision.HIGHEST


def extend_all(field_now, send_rows):
    nt, values, parts, elems = field_now.shape
    send_table = send_rows.reshape(2, N_SPACE, -1)
    layer_size = send_table.shape[2]
    shape_rows = (nt, values, parts, layer_size)
    bottom = jnp.take_along_axis(field_now, jnp.broadcast_to(send_table[0][None, None], shape_rows), axis=3)
    upper_rows = jnp.take_along_axis(field_now, jnp.broadcast_to(send_table[1][None, None], shape_rows), axis=3)
    zero_rows = jnp.zeros((nt, values, 1, layer_size), jnp.float32)
    below_rows = jnp.concatenate([zero_rows, upper_rows[:, :, :-1]], axis=2)
    above_rows = jnp.concatenate([bottom[:, :, 1:], zero_rows], axis=2)
    return jnp.concatenate([field_now, below_rows, above_rows], axis=3)


def coupling(field_now, face_blocks, neighbor, send_rows):
    extended = extend_all(field_now, send_rows)
    face_sum = jnp.zeros_like(field_now)
    for face in range(6):
        gather_index = jnp.broadcast_to(jnp.maximum(neighbor[face], 0)[None, None], field_now.shape)
        picked = jnp.take_along_axis(extended, gather_index, axis=3)
        face_valid = (neighbor[face] >= 0).astype(jnp.float32)
        picked = picked * face_valid[None, None]
        face_sum = face_sum + jnp.einsum("ij,tjse->tise", face_blocks[face], picked, precision=HIGHEST_PRECISION)
    return face_sum


def reference(initial_state, forcing, coarse_gain, block_inverse, face_blocks, neighbor, send_rows):
    values = initial_state.shape[0]
    nt = coarse_gain.shape[0]
    parts = N_SPACE
    elems = initial_state.shape[1] // parts
    start_field = initial_state.reshape(values, parts, elems)
    sources = forcing.reshape(nt, STEPS, values, parts, elems)
    gain_factors = coarse_gain.reshape(nt, values, parts, elems)
    inverse = block_inverse.reshape(values, values, parts, elems)
    adjacency = neighbor.reshape(6, parts, elems)

    def apply_inverse(vector):
        return jnp.einsum("ijse,tjse->tise", inverse, vector, precision=HIGHEST_PRECISION)

    coarse = jnp.zeros((nt, values, parts, elems), jnp.float32)
    residual = coarse
    for iteration in range(ITERS):
        field_now = jnp.concatenate([start_field[None], coarse[:-1]], axis=0)
        for step_index in range(STEPS):
            right_side = field_now + sources[:, step_index]
            field_now = apply_inverse(right_side)
            for sweep_index in range(SWEEPS):
                field_now = apply_inverse(right_side - coupling(field_now, face_blocks, adjacency, send_rows))
        residual = field_now - coarse

        def chain(running, pair):
            running = pair[0] * running + pair[1]
            return running, running

        zero_field = jnp.zeros((values, parts, elems), jnp.float32)
        running, correction = lax.scan(chain, zero_field, (gain_factors, residual))
        coarse = coarse + correction
    shape_out = (nt, values, parts * elems)
    return coarse.reshape(shape_out), residual.reshape(shape_out)
```

```python
import functools

import jax
import jax.numpy as jnp
from jax import lax
from jax.experimental import pallas as pl
from jax.experimental.pallas import tpu as pltpu
from jax.sharding import PartitionSpec as P

SWEEPS = 2
ITERS = 2
LANES = 128
SUB = 8
MESH = pl.DeviceIdType.MESH


def pick(block, index):
    return jnp.concatenate(
        [
            jnp.take_along_axis(block[r : r + SUB], index, axis=1, mode="promise_in_bounds")
            for r in range(0, block.shape[0], SUB)
        ],
        axis=0,
    )


def masked(value, mask):
    return jnp.concatenate(
        [jnp.where(mask, value[r : r + SUB], 0.0) for r in range(0, value.shape[0], SUB)], axis=0
    )


def kernel(
    tm, ns, steps,
    init_ref, forcing_ref, gain_ref, inverse_ref, faces_ref, neighbor_ref, send_rows_ref,
    coarse_ref, residual_ref,
    inv_t, wide, f_ref, r_ref, idx_ref,
    send_up, send_dn, below, above,
    gbuf, rbuf, cbuf, cin,
    up_send, up_recv, dn_send, dn_recv,
    g_send, g_recv, a_send, a_recv, c_send, c_recv,
):
    values, elems = init_ref.shape
    layer = elems // 2
    half = values // 2
    scanners = min(tm, values // SUB)
    rows = values // scanners
    k = lax.axis_index("tm")
    p = lax.axis_index("space")

    barrier = pltpu.get_barrier_semaphore()
    for d in range(1, tm):
        pl.semaphore_signal(barrier, inc=1, device_id=(lax.rem(k + d, tm), p), device_id_type=MESH)

    @pl.when(p > 0)
    def _():
        pl.semaphore_signal(barrier, inc=1, device_id=(k, p - 1), device_id_type=MESH)

    @pl.when(p < ns - 1)
    def _():
        pl.semaphore_signal(barrier, inc=1, device_id=(k, p + 1), device_id_type=MESH)

    def turn(j, carry):
        for i in range(0, values, SUB):
            inv_t[j, pl.ds(i, SUB), :] = inverse_ref[pl.ds(i * values + j, SUB, stride=values), :]
        return carry

    lax.fori_loop(0, values, turn, 0, unroll=4)

    for f in range(6):
        part = faces_ref[(4, 5, 0, 1, 2, 3)[f]]
        high = part.astype(jnp.bfloat16).astype(jnp.float32)
        low = part - high
        for c, piece in enumerate((high, low, high, low)):
            wide[f * values : (f + 1) * values, c * values : (c + 1) * values] = piece
    f_ref[...] = wide[...].astype(jnp.bfloat16)

    for row in range(2):
        for at in (0, layer):
            idx_ref[row : row + 1, at : at + layer] = send_rows_ref[row : row + 1, :]

    def spread(row):
        return jnp.broadcast_to(row, (SUB, LANES))

    low_index = spread(idx_ref[0:1, :])
    high_index = spread(idx_ref[1:2, :])
    lane = lax.broadcasted_iota(jnp.int32, (SUB, LANES), 1)
    first_half = lane < layer
    side = [spread(neighbor_ref[f : f + 1, :]) for f in range(6)]
    own_mask = [(n >= 0) & (n < elems) for n in side]
    own_index = [jnp.clip(n, 0, elems - 1) for n in side]
    halo_mask, halo_index = [], []
    for n, base in ((side[4], elems), (side[5], elems + layer)):
        halo_mask.append((n >= base) & (n < base + layer))
        halo_index.append(jnp.clip(n - base, 0, layer - 1))

    @pl.when(p == 0)
    def _():
        below[...] = jnp.zeros_like(below)

    @pl.when(p == ns - 1)
    def _():
        above[...] = jnp.zeros_like(above)

    expected = tm - 1 + (p > 0).astype(jnp.int32) + (p < ns - 1).astype(jnp.int32)
    pl.semaphore_wait(barrier, expected)

    def when_scanner(place, run):
        if scanners == tm:
            run()
        else:
            pl.when(place < scanners)(run)

    def to_scanner(src, dst, d, send, recv):
        place = lax.rem(k + d, tm)
        return pltpu.make_async_remote_copy(
            src_ref=src.at[pl.ds(pl.multiple_of(lax.rem(place, scanners) * rows, SUB), rows)],
            dst_ref=dst.at[k], send_sem=send.at[d], recv_sem=recv.at[d],
            device_id=(place, p), device_id_type=MESH,
        )

    def from_scanner(d):
        place = lax.rem(k + d, tm)
        return pltpu.make_async_remote_copy(
            src_ref=cbuf.at[place],
            dst_ref=cin.at[pl.ds(pl.multiple_of(lax.rem(k, scanners) * rows, SUB), rows)],
            send_sem=c_send.at[d], recv_sem=c_recv.at[d],
            device_id=(place, p), device_id_type=MESH,
        )

    my_rows = pl.ds(pl.multiple_of(lax.rem(k, scanners) * rows, SUB), rows)
    gains = gain_ref.at[0]
    for d in range(1, tm):
        when_scanner(lax.rem(k + d, tm), lambda d=d: to_scanner(gains, gbuf, d, g_send, g_recv).start())

    def apply_inverse(vector):
        r_ref[...] = vector
        sums = [None, None]
        for j in range(values):
            term = inv_t[j] * r_ref[j : j + 1, :]
            sums[j % 2] = term if sums[j % 2] is None else sums[j % 2] + term
        return sums[0] + sums[1]

    def up_copy(s):
        return pltpu.make_async_remote_copy(
            src_ref=send_up.at[s], dst_ref=below.at[s], send_sem=up_send.at[s],
            recv_sem=up_recv.at[s], device_id=(k, p + 1), device_id_type=MESH,
        )

    def dn_copy(s):
        return pltpu.make_async_remote_copy(
            src_ref=send_dn.at[s], dst_ref=above.at[s], send_sem=dn_send.at[s],
            recv_sem=dn_recv.at[s], device_id=(k, p - 1), device_id_type=MESH,
        )

    def packed(block, index):
        halves = [pick(block[:half], index), pick(block[half:], index)]
        return jnp.concatenate(
            [
                jnp.where(first_half, halves[0][r : r + SUB], halves[1][r : r + SUB])
                for r in range(0, half, SUB)
            ],
            axis=0,
        )

    def unpacked(block, index, mask):
        return masked(
            jnp.concatenate([pick(block, index), pick(block, index + layer)], axis=0), mask
        )

    def remainder(x, b, s):
        high = x.astype(jnp.bfloat16)
        low = (x - high.astype(jnp.float32)).astype(jnp.bfloat16)
        stack = jnp.concatenate([high, high, low, low], axis=0)
        along_z = jnp.dot(
            f_ref[: 2 * values, :], stack, preferred_element_type=jnp.float32
        )
        minus_z, plus_z = along_z[:values], along_z[values:]
        send_up[s] = packed(minus_z, high_index)
        send_dn[s] = packed(plus_z, low_index)

        @pl.when(p < ns - 1)
        def _():
            up_copy(s).start()

        @pl.when(p > 0)
        def _():
            dn_copy(s).start()

        along_xy = jnp.dot(
            f_ref[2 * values :, :], stack, preferred_element_type=jnp.float32
        )
        rest = b - masked(pick(minus_z, own_index[4]), own_mask[4])
        rest = rest - masked(pick(plus_z, own_index[5]), own_mask[5])
        for f in range(4):
            product = along_xy[f * values : (f + 1) * values]
            rest = rest - masked(pick(product, own_index[f]), own_mask[f])

        @pl.when(p < ns - 1)
        def _():
            up_copy(s).wait_send()
            dn_copy(s).wait_recv()

        @pl.when(p > 0)
        def _():
            dn_copy(s).wait_send()
            up_copy(s).wait_recv()

        rest = rest - unpacked(below[s], halo_index[0], halo_mask[0])
        return rest - unpacked(above[s], halo_index[1], halo_mask[1])

    def fine_step(m, field):
        b = field + forcing_ref[m]
        x = apply_inverse(b)
        for sweep in range(SWEEPS):
            x = apply_inverse(remainder(x, b, sweep % 2))
        return x

    def carried_in(first):
        res = residual_ref.at[0]
        for d in range(1, tm):
            when_scanner(
                lax.rem(k + d, tm), lambda d=d: to_scanner(res, rbuf, d, a_send, a_recv).start()
            )

        def scan():
            rbuf[k] = res[my_rows, :]
            if first:
                gbuf[k] = gains[my_rows, :]
                for d in range(1, tm):
                    to_scanner(gains, gbuf, d, g_send, g_recv).wait_recv()
            for d in range(1, tm):
                to_scanner(res, rbuf, d, a_send, a_recv).wait_recv()
            running = jnp.zeros((rows, LANES), jnp.float32)
            for lap in range(tm):
                cbuf[lap] = running
                running = gbuf[lap] * running + rbuf[lap]
            for d in range(1, tm):
                from_scanner(d).start()
            cin[my_rows, :] = cbuf[k]

        when_scanner(k, scan)
        for d in range(1, tm):

            def sent(d=d):
                if first:
                    to_scanner(gains, gbuf, d, g_send, g_recv).wait_send()
                to_scanner(res, rbuf, d, a_send, a_recv).wait_send()

            when_scanner(lax.rem(k + d, tm), sent)
            when_scanner(lax.rem(k + tm - d, tm), lambda d=d: from_scanner(d).wait_recv())

        def returned():
            for d in range(1, tm):
                from_scanner(d).wait_send()

        when_scanner(k, returned)
        return cin[...]

    coarse = jnp.zeros((values, elems), jnp.float32)
    previous = coarse
    for iteration in range(ITERS):
        field = lax.fori_loop(
            0, steps, fine_step, jnp.where(k == 0, init_ref[...], previous)
        )
        residual = field - coarse
        residual_ref[0] = residual
        carried = carried_in(iteration == 0)
        previous = previous + carried
        coarse = coarse + (gain_ref[0] * carried + residual)
    coarse_ref[0] = coarse


def body(tm, ns, initial_state, forcing, coarse_gain, block_inverse, face_blocks, neighbor, send_rows):
    values, elems = initial_state.shape
    steps = forcing.shape[0]
    scanners = min(tm, values // SUB)
    rows = values // scanners
    f32 = jnp.float32
    out = jax.ShapeDtypeStruct((1, values, elems), f32)
    vmem = pl.BlockSpec(memory_space=pltpu.VMEM)
    dma = pltpu.SemaphoreType.DMA
    return tuple(
        pl.pallas_call(
            functools.partial(kernel, tm, ns, steps),
            out_shape=(out, out),
            in_specs=[vmem] * 7,
            out_specs=(vmem, vmem),
            scratch_shapes=[
                pltpu.VMEM((values, values, elems), f32),
                pltpu.VMEM((6 * values, 4 * values), f32),
                pltpu.VMEM((6 * values, 4 * values), jnp.bfloat16),
                pltpu.VMEM((values, elems), f32),
                pltpu.VMEM((SUB, elems), jnp.int32),
                pltpu.VMEM((2, values // 2, elems), f32),
                pltpu.VMEM((2, values // 2, elems), f32),
                pltpu.VMEM((2, values // 2, elems), f32),
                pltpu.VMEM((2, values // 2, elems), f32),
                pltpu.VMEM((tm, rows, elems), f32),
                pltpu.VMEM((tm, rows, elems), f32),
                pltpu.VMEM((tm, rows, elems), f32),
                pltpu.VMEM((values, elems), f32),
                dma((2,)), dma((2,)), dma((2,)), dma((2,)),
                dma((tm,)), dma((tm,)), dma((tm,)), dma((tm,)), dma((tm,)), dma((tm,)),
            ],
            compiler_params=pltpu.CompilerParams(
                collective_id=0, has_side_effects=True, vmem_limit_bytes=32 * 1024 * 1024
            ),
        )(
            initial_state, forcing, coarse_gain,
            block_inverse.reshape(values * values, elems), face_blocks, neighbor, send_rows,
        )
    )


def solution(mesh):
    return jax.shard_map(
        functools.partial(body, mesh.shape["tm"], mesh.shape["space"]),
        mesh=mesh,
        in_specs=(
            P(None, "space"),
            P("tm", None, "space"),
            P("tm", None, "space"),
            P(None, None, "space"),
            P(),
            P(None, "space"),
            P(None, "space"),
        ),
        out_specs=(P("tm", None, "space"), P("tm", None, "space")),
        check_vma=False,
    )
```

```python
import functools

import jax
import jax.numpy as jnp
from jax import lax
from jax.experimental import pallas as pl
from jax.experimental.pallas import tpu as pltpu
from jax.sharding import PartitionSpec as P

SWEEPS = 2
ITERS = 2
LANES = 128
SUB = 8
MESH = pl.DeviceIdType.MESH


def pick(block, index):
    return jnp.concatenate(
        [
            jnp.take_along_axis(block[r : r + SUB], index, axis=1, mode="promise_in_bounds")
            for r in range(0, block.shape[0], SUB)
        ],
        axis=0,
    )


def masked(value, mask):
    return jnp.concatenate(
        [jnp.where(mask, value[r : r + SUB], 0.0) for r in range(0, value.shape[0], SUB)], axis=0
    )


def kernel(
    tm, ns, steps,
    init_hbm, forcing_hbm, gain_hbm, inverse_hbm, faces_hbm, neighbor_hbm, send_rows_hbm,
    out_ref,
    init_ref, forcing_ref, gain_ref, inverse_ref, faces_ref, neighbor_ref, send_rows_ref,
    load_sem, res,
    inv_t, wide, f_ref, r_ref, idx_ref,
    send_up, send_dn, below, above,
    gbuf, rbuf, cbuf, cin,
    up_send, up_recv, dn_send, dn_recv,
    g_send, g_recv, a_send, a_recv, c_send, c_recv,
):
    values, elems = init_ref.shape
    layer = elems // 2
    half = values // 2
    scanners = min(tm, values // SUB)
    rows = values // scanners
    k = lax.axis_index("tm")
    p = lax.axis_index("space")

    loads = [
        pltpu.make_async_copy(src, dst, load_sem.at[n])
        for n, (src, dst) in enumerate(
            (
                (inverse_hbm, inverse_ref),
                (faces_hbm, faces_ref),
                (neighbor_hbm, neighbor_ref),
                (send_rows_hbm, send_rows_ref),
                (init_hbm, init_ref),
                (forcing_hbm, forcing_ref),
                (gain_hbm, gain_ref),
            )
        )
    ]
    for load in loads:
        load.start()

    barrier = pltpu.get_barrier_semaphore()
    for d in range(1, tm):
        pl.semaphore_signal(barrier, inc=1, device_id=(lax.rem(k + d, tm), p), device_id_type=MESH)

    @pl.when(p > 0)
    def _():
        pl.semaphore_signal(barrier, inc=1, device_id=(k, p - 1), device_id_type=MESH)

    @pl.when(p < ns - 1)
    def _():
        pl.semaphore_signal(barrier, inc=1, device_id=(k, p + 1), device_id_type=MESH)

    for load in loads[1:]:
        load.wait()

    for f in range(6):
        part = faces_ref[(4, 5, 0, 1, 2, 3)[f]]
        high = part.astype(jnp.bfloat16).astype(jnp.float32)
        low = part - high
        for c, piece in enumerate((high, low, high, low)):
            wide[f * values : (f + 1) * values, c * values : (c + 1) * values] = piece
    f_ref[...] = wide[...].astype(jnp.bfloat16)

    for row in range(2):
        for at in (0, layer):
            idx_ref[row : row + 1, at : at + layer] = send_rows_ref[row : row + 1, :]

    def spread(row):
        return jnp.broadcast_to(row, (SUB, LANES))

    low_index = spread(idx_ref[0:1, :])
    high_index = spread(idx_ref[1:2, :])
    lane = lax.broadcasted_iota(jnp.int32, (SUB, LANES), 1)
    first_half = lane < layer
    side = [spread(neighbor_ref[f : f + 1, :]) for f in range(6)]
    own_mask = [(n >= 0) & (n < elems) for n in side]
    own_index = [jnp.clip(n, 0, elems - 1) for n in side]
    halo_mask, halo_index = [], []
    for n, base in ((side[4], elems), (side[5], elems + layer)):
        halo_mask.append((n >= base) & (n < base + layer))
        halo_index.append(jnp.clip(n - base, 0, layer - 1))

    @pl.when(p == 0)
    def _():
        below[...] = jnp.zeros_like(below)

    @pl.when(p == ns - 1)
    def _():
        above[...] = jnp.zeros_like(above)

    loads[0].wait()

    def turn(j, carry):
        for i in range(0, values, SUB):
            inv_t[j, pl.ds(i, SUB), :] = inverse_ref[pl.ds(i * values + j, SUB, stride=values), :]
        return carry

    lax.fori_loop(0, values, turn, 0, unroll=4)

    expected = tm - 1 + (p > 0).astype(jnp.int32) + (p < ns - 1).astype(jnp.int32)
    pl.semaphore_wait(barrier, expected)

    def when_scanner(place, run):
        if scanners == tm:
            run()
        else:
            pl.when(place < scanners)(run)

    def to_scanner(src, dst, d, send, recv):
        place = lax.rem(k + d, tm)
        return pltpu.make_async_remote_copy(
            src_ref=src.at[pl.ds(pl.multiple_of(lax.rem(place, scanners) * rows, SUB), rows)],
            dst_ref=dst.at[k], send_sem=send.at[d], recv_sem=recv.at[d],
            device_id=(place, p), device_id_type=MESH,
        )

    def from_scanner(d):
        place = lax.rem(k + d, tm)
        return pltpu.make_async_remote_copy(
            src_ref=cbuf.at[place],
            dst_ref=cin.at[pl.ds(pl.multiple_of(lax.rem(k, scanners) * rows, SUB), rows)],
            send_sem=c_send.at[d], recv_sem=c_recv.at[d],
            device_id=(place, p), device_id_type=MESH,
        )

    my_rows = pl.ds(pl.multiple_of(lax.rem(k, scanners) * rows, SUB), rows)
    gains = gain_ref.at[0]
    for d in range(1, tm):
        when_scanner(lax.rem(k + d, tm), lambda d=d: to_scanner(gains, gbuf, d, g_send, g_recv).start())

    def apply_inverse(vector):
        r_ref[...] = vector
        sums = [None, None]
        for j in range(values):
            term = inv_t[j] * r_ref[j : j + 1, :]
            sums[j % 2] = term if sums[j % 2] is None else sums[j % 2] + term
        return sums[0] + sums[1]

    def up_copy(s):
        return pltpu.make_async_remote_copy(
            src_ref=send_up.at[s], dst_ref=below.at[s], send_sem=up_send.at[s],
            recv_sem=up_recv.at[s], device_id=(k, p + 1), device_id_type=MESH,
        )

    def dn_copy(s):
        return pltpu.make_async_remote_copy(
            src_ref=send_dn.at[s], dst_ref=above.at[s], send_sem=dn_send.at[s],
            recv_sem=dn_recv.at[s], device_id=(k, p - 1), device_id_type=MESH,
        )

    def packed(block, index):
        halves = [pick(block[:half], index), pick(block[half:], index)]
        return jnp.concatenate(
            [
                jnp.where(first_half, halves[0][r : r + SUB], halves[1][r : r + SUB])
                for r in range(0, half, SUB)
            ],
            axis=0,
        )

    def unpacked(block, index, mask):
        return masked(
            jnp.concatenate([pick(block, index), pick(block, index + layer)], axis=0), mask
        )

    def sent_halo(s, also):
        @pl.when((p < ns - 1) & also)
        def _():
            up_copy(s).wait_send()

        @pl.when((p > 0) & also)
        def _():
            dn_copy(s).wait_send()

    def remainder(x, b, s):
        high = x.astype(jnp.bfloat16)
        low = (x - high.astype(jnp.float32)).astype(jnp.bfloat16)
        stack = jnp.concatenate([high, high, low, low], axis=0)
        along_z = jnp.dot(
            f_ref[: 2 * values, :], stack, preferred_element_type=jnp.float32
        )
        minus_z, plus_z = along_z[:values], along_z[values:]
        send_up[s] = packed(minus_z, high_index)
        send_dn[s] = packed(plus_z, low_index)

        @pl.when(p < ns - 1)
        def _():
            up_copy(s).start()

        @pl.when(p > 0)
        def _():
            dn_copy(s).start()

        along_xy = jnp.dot(
            f_ref[2 * values :, :], stack, preferred_element_type=jnp.float32
        )
        rest = b - masked(pick(minus_z, own_index[4]), own_mask[4])
        rest = rest - masked(pick(plus_z, own_index[5]), own_mask[5])
        for f in range(4):
            product = along_xy[f * values : (f + 1) * values]
            rest = rest - masked(pick(product, own_index[f]), own_mask[f])

        @pl.when(p < ns - 1)
        def _():
            dn_copy(s).wait_recv()

        @pl.when(p > 0)
        def _():
            up_copy(s).wait_recv()

        rest = rest - unpacked(below[s], halo_index[0], halo_mask[0])
        return rest - unpacked(above[s], halo_index[1], halo_mask[1])

    def fine_step(m, field):
        b = field + forcing_ref[m]
        x = apply_inverse(b)
        for sweep in range(SWEEPS):
            rest = remainder(x, b, sweep)
            if sweep == 0:
                sent_halo(SWEEPS - 1, m > 0)
            else:
                sent_halo(sweep - 1, True)
            x = apply_inverse(rest)
        return x

    def carried_in(first):
        for d in range(1, tm):
            when_scanner(
                lax.rem(k + d, tm), lambda d=d: to_scanner(res, rbuf, d, a_send, a_recv).start()
            )

        def scan():
            rbuf[k] = res[my_rows, :]
            if first:
                gbuf[k] = gains[my_rows, :]
                for d in range(1, tm):
                    to_scanner(gains, gbuf, d, g_send, g_recv).wait_recv()
            for d in range(1, tm):
                to_scanner(res, rbuf, d, a_send, a_recv).wait_recv()
            running = jnp.zeros((rows, LANES), jnp.float32)
            for lap in range(tm):
                cbuf[lap] = running
                running = gbuf[lap] * running + rbuf[lap]
            for d in range(1, tm):
                from_scanner(d).start()
            cin[my_rows, :] = cbuf[k]

        when_scanner(k, scan)
        for d in range(1, tm):

            def sent(d=d):
                if first:
                    to_scanner(gains, gbuf, d, g_send, g_recv).wait_send()
                to_scanner(res, rbuf, d, a_send, a_recv).wait_send()

            when_scanner(lax.rem(k + d, tm), sent)
            when_scanner(lax.rem(k + tm - d, tm), lambda d=d: from_scanner(d).wait_recv())

        def returned():
            for d in range(1, tm):
                from_scanner(d).wait_send()

        when_scanner(k, returned)
        return cin[...]

    coarse = jnp.zeros((values, elems), jnp.float32)
    previous = coarse
    for iteration in range(ITERS):
        field = lax.fori_loop(
            0, steps, fine_step, jnp.where(k == 0, init_ref[...], previous)
        )
        sent_halo(SWEEPS - 1, True)
        residual = field - coarse
        res[...] = residual
        carried = carried_in(iteration == 0)
        previous = previous + carried
        coarse = coarse + (gain_ref[0] * carried + residual)
    out_ref[0] = coarse
    out_ref[1] = residual


def body(tm, ns, initial_state, forcing, coarse_gain, block_inverse, face_blocks, neighbor, send_rows):
    values, elems = initial_state.shape
    steps = forcing.shape[0]
    scanners = min(tm, values // SUB)
    rows = values // scanners
    f32 = jnp.float32
    out = jax.ShapeDtypeStruct((2, values, elems), f32)
    vmem = pl.BlockSpec(memory_space=pltpu.VMEM)
    dma = pltpu.SemaphoreType.DMA
    both = (
        pl.pallas_call(
            functools.partial(kernel, tm, ns, steps),
            out_shape=out,
            in_specs=[pl.BlockSpec(memory_space=pl.ANY)] * 7,
            out_specs=vmem,
            scratch_shapes=[
                pltpu.VMEM((values, elems), f32),
                pltpu.VMEM(forcing.shape, f32),
                pltpu.VMEM((1, values, elems), f32),
                pltpu.VMEM((values * values, elems), f32),
                pltpu.VMEM(face_blocks.shape, f32),
                pltpu.VMEM(neighbor.shape, jnp.int32),
                pltpu.VMEM(send_rows.shape, jnp.int32),
                dma((7,)),
                pltpu.VMEM((values, elems), f32),
                pltpu.VMEM((values, values, elems), f32),
                pltpu.VMEM((6 * values, 4 * values), f32),
                pltpu.VMEM((6 * values, 4 * values), jnp.bfloat16),
                pltpu.VMEM((values, elems), f32),
                pltpu.VMEM((SUB, elems), jnp.int32),
                pltpu.VMEM((2, values // 2, elems), f32),
                pltpu.VMEM((2, values // 2, elems), f32),
                pltpu.VMEM((2, values // 2, elems), f32),
                pltpu.VMEM((2, values // 2, elems), f32),
                pltpu.VMEM((tm, rows, elems), f32),
                pltpu.VMEM((tm, rows, elems), f32),
                pltpu.VMEM((tm, rows, elems), f32),
                pltpu.VMEM((values, elems), f32),
                dma((2,)), dma((2,)), dma((2,)), dma((2,)),
                dma((tm,)), dma((tm,)), dma((tm,)), dma((tm,)), dma((tm,)), dma((tm,)),
            ],
            compiler_params=pltpu.CompilerParams(
                collective_id=0, has_side_effects=True, vmem_limit_bytes=63 * 1024 * 1024
            ),
        )(
            initial_state, forcing, coarse_gain,
            block_inverse.reshape(values * values, elems), face_blocks, neighbor, send_rows,
        )
    )
    return both[:1], both[1:]


def solution(mesh):
    return jax.shard_map(
        functools.partial(body, mesh.shape["tm"], mesh.shape["space"]),
        mesh=mesh,
        in_specs=(
            P(None, "space"),
            P("tm", None, "space"),
            P("tm", None, "space"),
            P(None, None, "space"),
            P(),
            P(None, "space"),
            P(None, "space"),
        ),
        out_specs=(P("tm", None, "space"), P("tm", None, "space")),
        check_vma=False,
    )
```

```python
import functools

import jax
import jax.numpy as jnp
from jax import lax
from jax.experimental import pallas as pl
from jax.experimental.pallas import tpu as pltpu
from jax.sharding import PartitionSpec as P

SWEEPS = 2
ITERS = 2
LANES = 128
SUB = 8
MESH = pl.DeviceIdType.MESH


def pick(block, index):
    return jnp.concatenate(
        [
            jnp.take_along_axis(block[r : r + SUB], index, axis=1, mode="promise_in_bounds")
            for r in range(0, block.shape[0], SUB)
        ],
        axis=0,
    )


def masked(value, mask):
    return jnp.concatenate(
        [jnp.where(mask, value[r : r + SUB], 0.0) for r in range(0, value.shape[0], SUB)], axis=0
    )


def kernel(
    tm, ns, steps,
    init_hbm, forcing_hbm, gain_hbm, inverse_hbm, faces_hbm, neighbor_hbm, send_rows_hbm,
    out_ref,
    init_ref, forcing_ref, gain_ref, inverse_ref, faces_ref, neighbor_ref, send_rows_ref,
    load_sem, res,
    inv_t, halo_inv_t, wide, f_ref, r_ref, idx_ref,
    up_blocks, dn_blocks, below_blocks, above_blocks,
    send_up, send_dn, below, above,
    gbuf, rbuf, cbuf, cin,
    up_send, up_recv, dn_send, dn_recv,
    ub_send, ub_recv, db_send, db_recv,
    g_send, g_recv, a_send, a_recv, c_send, c_recv,
):
    values, elems = init_ref.shape
    layer = elems // 2
    half = values // 2
    scanners = min(tm, values // SUB)
    rows = values // scanners
    k = lax.axis_index("tm")
    p = lax.axis_index("space")

    loads = [
        pltpu.make_async_copy(src, dst, load_sem.at[n])
        for n, (src, dst) in enumerate(
            (
                (inverse_hbm, inverse_ref),
                (faces_hbm, faces_ref),
                (neighbor_hbm, neighbor_ref),
                (send_rows_hbm, send_rows_ref),
                (init_hbm, init_ref),
                (forcing_hbm, forcing_ref),
                (gain_hbm, gain_ref),
            )
        )
    ]
    for load in loads:
        load.start()

    barrier = pltpu.get_barrier_semaphore()
    for d in range(1, tm):
        pl.semaphore_signal(barrier, inc=1, device_id=(lax.rem(k + d, tm), p), device_id_type=MESH)

    @pl.when(p > 0)
    def _():
        pl.semaphore_signal(barrier, inc=1, device_id=(k, p - 1), device_id_type=MESH)

    @pl.when(p < ns - 1)
    def _():
        pl.semaphore_signal(barrier, inc=1, device_id=(k, p + 1), device_id_type=MESH)

    for load in loads[1:]:
        load.wait()

    for f in range(6):
        part = faces_ref[(4, 5, 0, 1, 2, 3)[f]]
        high = part.astype(jnp.bfloat16).astype(jnp.float32)
        low = part - high
        for c, piece in enumerate((high, low, high, low)):
            wide[f * values : (f + 1) * values, c * values : (c + 1) * values] = piece
    f_ref[...] = wide[...].astype(jnp.bfloat16)

    for row in range(2):
        for at in (0, layer):
            idx_ref[row : row + 1, at : at + layer] = send_rows_ref[row : row + 1, :]

    def spread(row):
        return jnp.broadcast_to(row, (SUB, LANES))

    low_index = spread(idx_ref[0:1, :])
    high_index = spread(idx_ref[1:2, :])
    lane = lax.broadcasted_iota(jnp.int32, (SUB, LANES), 1)
    first_half = lane < layer
    side = [spread(neighbor_ref[f : f + 1, :]) for f in range(6)]
    own_mask = [(n >= 0) & (n < elems) for n in side]
    own_index = [jnp.clip(n, 0, elems - 1) for n in side]
    halo_mask, halo_index = [], []
    for n, base in ((side[4], elems), (side[5], elems + layer)):
        halo_mask.append((n >= base) & (n < base + layer))
        halo_index.append(jnp.clip(n - base, 0, layer - 1))

    @pl.when(p == 0)
    def _():
        below[...] = jnp.zeros_like(below)
        below_blocks[...] = jnp.zeros_like(below_blocks)

    @pl.when(p == ns - 1)
    def _():
        above[...] = jnp.zeros_like(above)
        above_blocks[...] = jnp.zeros_like(above_blocks)

    loads[0].wait()

    def turn(j, carry):
        for i in range(0, values, SUB):
            inv_t[j, pl.ds(i, SUB), :] = inverse_ref[pl.ds(i * values + j, SUB, stride=values), :]
        return carry

    lax.fori_loop(0, values, turn, 0, unroll=4)

    expected = tm - 1 + (p > 0).astype(jnp.int32) + (p < ns - 1).astype(jnp.int32)
    pl.semaphore_wait(barrier, expected)

    def when_scanner(place, run):
        if scanners == tm:
            run()
        else:
            pl.when(place < scanners)(run)

    def to_scanner(src, dst, d, send, recv):
        place = lax.rem(k + d, tm)
        return pltpu.make_async_remote_copy(
            src_ref=src.at[pl.ds(pl.multiple_of(lax.rem(place, scanners) * rows, SUB), rows)],
            dst_ref=dst.at[k], send_sem=send.at[d], recv_sem=recv.at[d],
            device_id=(place, p), device_id_type=MESH,
        )

    def from_scanner(d):
        place = lax.rem(k + d, tm)
        return pltpu.make_async_remote_copy(
            src_ref=cbuf.at[place],
            dst_ref=cin.at[pl.ds(pl.multiple_of(lax.rem(k, scanners) * rows, SUB), rows)],
            send_sem=c_send.at[d], recv_sem=c_recv.at[d],
            device_id=(place, p), device_id_type=MESH,
        )

    my_rows = pl.ds(pl.multiple_of(lax.rem(k, scanners) * rows, SUB), rows)
    gains = gain_ref.at[0]
    for d in range(1, tm):
        when_scanner(lax.rem(k + d, tm), lambda d=d: to_scanner(gains, gbuf, d, g_send, g_recv).start())

    def apply_inverse(vector, table=inv_t):
        r_ref[...] = vector
        sums = [None, None]
        for j in range(values):
            term = table[j] * r_ref[j : j + 1, :]
            sums[j % 2] = term if sums[j % 2] is None else sums[j % 2] + term
        return sums[0] + sums[1]

    def up_copy(s):
        return pltpu.make_async_remote_copy(
            src_ref=send_up.at[s], dst_ref=below.at[s], send_sem=up_send.at[s],
            recv_sem=up_recv.at[s], device_id=(k, p + 1), device_id_type=MESH,
        )

    def dn_copy(s):
        return pltpu.make_async_remote_copy(
            src_ref=send_dn.at[s], dst_ref=above.at[s], send_sem=dn_send.at[s],
            recv_sem=dn_recv.at[s], device_id=(k, p - 1), device_id_type=MESH,
        )

    chunks = SWEEPS * steps
    chunk = half // chunks

    def up_blocks_copy(c):
        part = pl.ds(c * chunk, chunk)
        return pltpu.make_async_remote_copy(
            src_ref=up_blocks.at[part], dst_ref=below_blocks.at[part], send_sem=ub_send.at[c],
            recv_sem=ub_recv.at[c], device_id=(k, p + 1), device_id_type=MESH,
        )

    def dn_blocks_copy(c):
        part = pl.ds(c * chunk, chunk)
        return pltpu.make_async_remote_copy(
            src_ref=dn_blocks.at[part], dst_ref=above_blocks.at[part], send_sem=db_send.at[c],
            recv_sem=db_recv.at[c], device_id=(k, p - 1), device_id_type=MESH,
        )

    def packed(block, index):
        halves = [pick(block[:half], index), pick(block[half:], index)]
        return jnp.concatenate(
            [
                jnp.where(first_half, halves[0][r : r + SUB], halves[1][r : r + SUB])
                for r in range(0, half, SUB)
            ],
            axis=0,
        )

    def unpacked(block, index, mask):
        return masked(
            jnp.concatenate([pick(block, index), pick(block, index + layer)], axis=0), mask
        )

    def sent_halo(s, also):
        @pl.when((p < ns - 1) & also)
        def _():
            up_copy(s).wait_send()

        @pl.when((p > 0) & also)
        def _():
            dn_copy(s).wait_send()

    def split(x):
        high = x.astype(jnp.bfloat16)
        low = (x - high.astype(jnp.float32)).astype(jnp.bfloat16)
        return jnp.concatenate([high, high, low, low], axis=0)

    def z_faces(stack):
        product = jnp.dot(f_ref[: 2 * values, :], stack, preferred_element_type=jnp.float32)
        return product[:values], product[values:]

    def send_halo(minus_z, plus_z, s):
        send_up[s] = packed(minus_z, high_index)
        send_dn[s] = packed(plus_z, low_index)

        @pl.when(p < ns - 1)
        def _():
            up_copy(s).start()

        @pl.when(p > 0)
        def _():
            dn_copy(s).start()

    def own_part(b, stack, minus_z, plus_z):
        along_xy = jnp.dot(f_ref[2 * values :, :], stack, preferred_element_type=jnp.float32)
        rest = b - masked(pick(minus_z, own_index[4]), own_mask[4])
        rest = rest - masked(pick(plus_z, own_index[5]), own_mask[5])
        for f in range(4):
            product = along_xy[f * values : (f + 1) * values]
            rest = rest - masked(pick(product, own_index[f]), own_mask[f])
        return rest

    def halo(s):
        @pl.when(p < ns - 1)
        def _():
            dn_copy(s).wait_recv()

        @pl.when(p > 0)
        def _():
            up_copy(s).wait_recv()

        return unpacked(below[s], halo_index[0], halo_mask[0]) + unpacked(
            above[s], halo_index[1], halo_mask[1]
        )

    def send_blocks(c):
        def one(n, carry):
            j = c * chunk + n
            first, second = inv_t[j], inv_t[j + half]
            for dst, index in ((up_blocks, high_index), (dn_blocks, low_index)):
                for r in range(0, values, SUB):
                    dst[j, r : r + SUB, :] = jnp.where(
                        first_half, pick(first[r : r + SUB], index), pick(second[r : r + SUB], index)
                    )
            return carry

        lax.fori_loop(0, chunk, one, 0, unroll=True)

        @pl.when(p < ns - 1)
        def _():
            up_blocks_copy(c).start()

        @pl.when(p > 0)
        def _():
            dn_blocks_copy(c).start()

    def take_blocks():
        for c in range(chunks):

            @pl.when(p < ns - 1)
            def _(c=c):
                up_blocks_copy(c).wait_send()
                dn_blocks_copy(c).wait_recv()

            @pl.when(p > 0)
            def _(c=c):
                dn_blocks_copy(c).wait_send()
                up_blocks_copy(c).wait_recv()

        def one(j, carry):
            under, over = below_blocks[j], above_blocks[j]
            for at in (0, 1):
                for r in range(0, values, SUB):
                    rows_of = slice(r, r + SUB)
                    over_part = jnp.where(
                        halo_mask[1], pick(over[rows_of], halo_index[1] + at * layer), 0.0
                    )
                    halo_inv_t[j + at * half, rows_of, :] = jnp.where(
                        halo_mask[0], pick(under[rows_of], halo_index[0] + at * layer), over_part
                    )
            return carry

        lax.fori_loop(0, half, one, 0)

    def fine_step(m, field):
        b = field + forcing_ref[m]
        x = apply_inverse(b)
        for sweep in range(SWEEPS):
            stack = split(x)
            minus_z, plus_z = z_faces(stack)
            send_halo(minus_z, plus_z, sweep)
            send_blocks(m * SWEEPS + sweep)
            rest = own_part(b, stack, minus_z, plus_z) - halo(sweep)
            if sweep == 0:
                sent_halo(SWEEPS - 1, m > 0)
            else:
                sent_halo(sweep - 1, True)
            x = apply_inverse(rest)
        return x

    def both_sweeps(m, field):
        base = 2 * lax.rem(m + 1, 2)
        b = field + forcing_ref[m]
        x = apply_inverse(b)
        stack = split(x)
        minus_z, plus_z = z_faces(stack)
        send_halo(minus_z, plus_z, base)
        inner = apply_inverse(own_part(b, stack, minus_z, plus_z))
        inner_minus, inner_plus = z_faces(split(inner))
        send_halo(inner_minus, inner_plus, base + 1)
        back = jnp.concatenate(
            [
                jnp.where(halo_mask[0], plus_z[r : r + SUB], minus_z[r : r + SUB])
                for r in range(0, values, SUB)
            ],
            axis=0,
        )
        back_minus, back_plus = z_faces(split(apply_inverse(back, halo_inv_t)))
        back = masked(back_minus, halo_mask[0]) + masked(back_plus, halo_mask[1])
        x = inner - apply_inverse(halo(base))
        stack = split(x)
        minus_z, plus_z = z_faces(stack)
        rest = own_part(b, stack, minus_z, plus_z) + back
        x = apply_inverse(rest - halo(base + 1))
        sent_halo(base, True)
        sent_halo(base + 1, True)
        return x

    def carried_in(first):
        for d in range(1, tm):
            when_scanner(
                lax.rem(k + d, tm), lambda d=d: to_scanner(res, rbuf, d, a_send, a_recv).start()
            )

        if first:
            take_blocks()

        def scan():
            rbuf[k] = res[my_rows, :]
            if first:
                gbuf[k] = gains[my_rows, :]
                for d in range(1, tm):
                    to_scanner(gains, gbuf, d, g_send, g_recv).wait_recv()
            for d in range(1, tm):
                to_scanner(res, rbuf, d, a_send, a_recv).wait_recv()
            running = jnp.zeros((rows, LANES), jnp.float32)
            for lap in range(tm):
                cbuf[lap] = running
                running = gbuf[lap] * running + rbuf[lap]
            for d in range(1, tm):
                from_scanner(d).start()
            cin[my_rows, :] = cbuf[k]

        when_scanner(k, scan)
        for d in range(1, tm):

            def sent(d=d):
                if first:
                    to_scanner(gains, gbuf, d, g_send, g_recv).wait_send()
                to_scanner(res, rbuf, d, a_send, a_recv).wait_send()

            when_scanner(lax.rem(k + d, tm), sent)
            when_scanner(lax.rem(k + tm - d, tm), lambda d=d: from_scanner(d).wait_recv())

        def returned():
            for d in range(1, tm):
                from_scanner(d).wait_send()

        when_scanner(k, returned)
        return cin[...]

    coarse = jnp.zeros((values, elems), jnp.float32)
    previous = coarse
    for iteration in range(ITERS):
        field = lax.fori_loop(
            0, steps, fine_step if iteration == 0 else both_sweeps, jnp.where(k == 0, init_ref[...], previous)
        )
        if iteration == 0:
            sent_halo(SWEEPS - 1, True)
        residual = field - coarse
        res[...] = residual
        carried = carried_in(iteration == 0)
        previous = previous + carried
        coarse = coarse + (gain_ref[0] * carried + residual)
    out_ref[0] = coarse
    out_ref[1] = residual


def body(tm, ns, initial_state, forcing, coarse_gain, block_inverse, face_blocks, neighbor, send_rows):
    values, elems = initial_state.shape
    steps = forcing.shape[0]
    scanners = min(tm, values // SUB)
    rows = values // scanners
    chunks = SWEEPS * steps
    f32 = jnp.float32
    out = jax.ShapeDtypeStruct((2, values, elems), f32)
    vmem = pl.BlockSpec(memory_space=pltpu.VMEM)
    dma = pltpu.SemaphoreType.DMA
    both = (
        pl.pallas_call(
            functools.partial(kernel, tm, ns, steps),
            out_shape=out,
            in_specs=[pl.BlockSpec(memory_space=pl.ANY)] * 7,
            out_specs=vmem,
            scratch_shapes=[
                pltpu.VMEM((values, elems), f32),
                pltpu.VMEM(forcing.shape, f32),
                pltpu.VMEM((1, values, elems), f32),
                pltpu.VMEM((values * values, elems), f32),
                pltpu.VMEM(face_blocks.shape, f32),
                pltpu.VMEM(neighbor.shape, jnp.int32),
                pltpu.VMEM(send_rows.shape, jnp.int32),
                dma((7,)),
                pltpu.VMEM((values, elems), f32),
                pltpu.VMEM((values, values, elems), f32),
                pltpu.VMEM((values, values, elems), f32),
                pltpu.VMEM((6 * values, 4 * values), f32),
                pltpu.VMEM((6 * values, 4 * values), jnp.bfloat16),
                pltpu.VMEM((values, elems), f32),
                pltpu.VMEM((SUB, elems), jnp.int32),
                pltpu.VMEM((values // 2, values, elems), f32),
                pltpu.VMEM((values // 2, values, elems), f32),
                pltpu.VMEM((values // 2, values, elems), f32),
                pltpu.VMEM((values // 2, values, elems), f32),
                pltpu.VMEM((4, values // 2, elems), f32),
                pltpu.VMEM((4, values // 2, elems), f32),
                pltpu.VMEM((4, values // 2, elems), f32),
                pltpu.VMEM((4, values // 2, elems), f32),
                pltpu.VMEM((tm, rows, elems), f32),
                pltpu.VMEM((tm, rows, elems), f32),
                pltpu.VMEM((tm, rows, elems), f32),
                pltpu.VMEM((values, elems), f32),
                dma((4,)), dma((4,)), dma((4,)), dma((4,)),
                dma((chunks,)), dma((chunks,)), dma((chunks,)), dma((chunks,)),
                dma((tm,)), dma((tm,)), dma((tm,)), dma((tm,)), dma((tm,)), dma((tm,)),
            ],
            compiler_params=pltpu.CompilerParams(
                collective_id=0, has_side_effects=True, vmem_limit_bytes=63 * 1024 * 1024
            ),
        )(
            initial_state, forcing, coarse_gain,
            block_inverse.reshape(values * values, elems), face_blocks, neighbor, send_rows,
        )
    )
    return both[:1], both[1:]


def solution(mesh):
    return jax.shard_map(
        functools.partial(body, mesh.shape["tm"], mesh.shape["space"]),
        mesh=mesh,
        in_specs=(
            P(None, "space"),
            P("tm", None, "space"),
            P("tm", None, "space"),
            P(None, None, "space"),
            P(),
            P(None, "space"),
            P(None, "space"),
        ),
        out_specs=(P("tm", None, "space"), P("tm", None, "space")),
        check_vma=False,
    )
```

```python
import functools

import jax
import jax.numpy as jnp
from jax import lax
from jax.experimental import pallas as pl
from jax.experimental.pallas import tpu as pltpu
from jax.sharding import PartitionSpec as P

SWEEPS = 2
ITERS = 2
LANES = 128
SUB = 8
MESH = pl.DeviceIdType.MESH


def pick(block, index):
    return jnp.concatenate(
        [
            jnp.take_along_axis(block[r : r + SUB], index, axis=1, mode="promise_in_bounds")
            for r in range(0, block.shape[0], SUB)
        ],
        axis=0,
    )


def masked(value, mask):
    return jnp.concatenate(
        [jnp.where(mask, value[r : r + SUB], 0.0) for r in range(0, value.shape[0], SUB)], axis=0
    )


def kernel(
    tm, ns, steps,
    init_hbm, forcing_hbm, gain_hbm, inverse_hbm, faces_hbm, neighbor_hbm, send_rows_hbm,
    out_ref,
    init_ref, forcing_ref, gain_ref, inverse_ref, faces_ref, neighbor_ref, send_rows_ref,
    load_sem, res,
    inv_t, halo_inv_t, wide, f_ref, r_ref, idx_ref,
    up_blocks, dn_blocks, below_blocks, above_blocks,
    send_up, send_dn, below, above,
    gbuf, rbuf, cbuf, cin,
    up_send, up_recv, dn_send, dn_recv,
    ub_send, ub_recv, db_send, db_recv,
    fu_send, fu_recv, fd_send, fd_recv,
    g_send, g_recv, a_send, a_recv, c_send, c_recv,
):
    values, elems = init_ref.shape
    layer = elems // 2
    half = values // 2
    scanners = min(tm, values // SUB)
    rows = values // scanners
    k = lax.axis_index("tm")
    p = lax.axis_index("space")

    loads = [
        pltpu.make_async_copy(src, dst, load_sem.at[n])
        for n, (src, dst) in enumerate(
            (
                (inverse_hbm, inverse_ref),
                (faces_hbm, faces_ref),
                (neighbor_hbm, neighbor_ref),
                (send_rows_hbm, send_rows_ref),
                (init_hbm, init_ref),
                (forcing_hbm, forcing_ref),
                (gain_hbm, gain_ref),
            )
        )
    ]
    for load in loads:
        load.start()

    barrier = pltpu.get_barrier_semaphore()
    for d in range(1, tm):
        pl.semaphore_signal(barrier, inc=1, device_id=(lax.rem(k + d, tm), p), device_id_type=MESH)

    @pl.when(p > 0)
    def _():
        pl.semaphore_signal(barrier, inc=1, device_id=(k, p - 1), device_id_type=MESH)

    @pl.when(p < ns - 1)
    def _():
        pl.semaphore_signal(barrier, inc=1, device_id=(k, p + 1), device_id_type=MESH)

    for load in loads[1:]:
        load.wait()

    for f in range(6):
        part = faces_ref[(4, 5, 0, 1, 2, 3)[f]]
        high = part.astype(jnp.bfloat16).astype(jnp.float32)
        low = part - high
        for c, piece in enumerate((high, low, high, low)):
            wide[f * values : (f + 1) * values, c * values : (c + 1) * values] = piece
    f_ref[...] = wide[...].astype(jnp.bfloat16)

    for row in range(2):
        for at in (0, layer):
            idx_ref[row : row + 1, at : at + layer] = send_rows_ref[row : row + 1, :]

    def spread(row):
        return jnp.broadcast_to(row, (SUB, LANES))

    low_index = spread(idx_ref[0:1, :])
    high_index = spread(idx_ref[1:2, :])
    lane = lax.broadcasted_iota(jnp.int32, (SUB, LANES), 1)
    first_half = lane < layer
    side = [spread(neighbor_ref[f : f + 1, :]) for f in range(6)]
    own_mask = [(n >= 0) & (n < elems) for n in side]
    own_index = [jnp.clip(n, 0, elems - 1) for n in side]
    halo_mask, halo_index = [], []
    for n, base in ((side[4], elems), (side[5], elems + layer)):
        halo_mask.append((n >= base) & (n < base + layer))
        halo_index.append(jnp.clip(n - base, 0, layer - 1))

    @pl.when(p == 0)
    def _():
        below[...] = jnp.zeros_like(below)
        below_blocks[...] = jnp.zeros_like(below_blocks)

    @pl.when(p == ns - 1)
    def _():
        above[...] = jnp.zeros_like(above)
        above_blocks[...] = jnp.zeros_like(above_blocks)

    loads[0].wait()

    def turn(j, carry):
        for i in range(0, values, SUB):
            inv_t[j, pl.ds(i, SUB), :] = inverse_ref[pl.ds(i * values + j, SUB, stride=values), :]
        return carry

    lax.fori_loop(0, values, turn, 0, unroll=4)

    expected = tm - 1 + (p > 0).astype(jnp.int32) + (p < ns - 1).astype(jnp.int32)
    pl.semaphore_wait(barrier, expected)

    def when_scanner(place, run):
        if scanners == tm:
            run()
        else:
            pl.when(place < scanners)(run)

    def to_scanner(src, dst, d, send, recv):
        place = lax.rem(k + d, tm)
        return pltpu.make_async_remote_copy(
            src_ref=src.at[pl.ds(pl.multiple_of(lax.rem(place, scanners) * rows, SUB), rows)],
            dst_ref=dst.at[k], send_sem=send.at[d], recv_sem=recv.at[d],
            device_id=(place, p), device_id_type=MESH,
        )

    def from_scanner(d):
        place = lax.rem(k + d, tm)
        return pltpu.make_async_remote_copy(
            src_ref=cbuf.at[place],
            dst_ref=cin.at[pl.ds(pl.multiple_of(lax.rem(k, scanners) * rows, SUB), rows)],
            send_sem=c_send.at[d], recv_sem=c_recv.at[d],
            device_id=(place, p), device_id_type=MESH,
        )

    my_rows = pl.ds(pl.multiple_of(lax.rem(k, scanners) * rows, SUB), rows)
    gains = gain_ref.at[0]
    for d in range(1, tm):
        when_scanner(lax.rem(k + d, tm), lambda d=d: to_scanner(gains, gbuf, d, g_send, g_recv).start())

    def apply_inverse(vector, table=inv_t):
        r_ref[...] = vector
        sums = [None, None]
        for j in range(values):
            term = table[j] * r_ref[j : j + 1, :]
            sums[j % 2] = term if sums[j % 2] is None else sums[j % 2] + term
        return sums[0] + sums[1]

    def up_copy(s):
        return pltpu.make_async_remote_copy(
            src_ref=send_up.at[s], dst_ref=below.at[s], send_sem=up_send.at[s],
            recv_sem=up_recv.at[s], device_id=(k, p + 1), device_id_type=MESH,
        )

    def dn_copy(s):
        return pltpu.make_async_remote_copy(
            src_ref=send_dn.at[s], dst_ref=above.at[s], send_sem=dn_send.at[s],
            recv_sem=dn_recv.at[s], device_id=(k, p - 1), device_id_type=MESH,
        )

    chunks = SWEEPS * steps
    chunk = half // (2 * chunks)
    core = lax.rem(k, 2)
    partner = k + 1 - 2 * core

    def part_of(c):
        return pl.ds(core * (half // 2) + c * chunk, chunk)

    def hand_on(blocks, send, recv, c):
        part = part_of(c)
        return pltpu.make_async_remote_copy(
            src_ref=blocks.at[part], dst_ref=blocks.at[part], send_sem=send.at[c],
            recv_sem=recv.at[c], device_id=(partner, p), device_id_type=MESH,
        )

    def up_blocks_copy(c):
        part = part_of(c)
        return pltpu.make_async_remote_copy(
            src_ref=up_blocks.at[part], dst_ref=below_blocks.at[part], send_sem=ub_send.at[c],
            recv_sem=ub_recv.at[c], device_id=(k, p + 1), device_id_type=MESH,
        )

    def dn_blocks_copy(c):
        part = part_of(c)
        return pltpu.make_async_remote_copy(
            src_ref=dn_blocks.at[part], dst_ref=above_blocks.at[part], send_sem=db_send.at[c],
            recv_sem=db_recv.at[c], device_id=(k, p - 1), device_id_type=MESH,
        )

    def packed(block, index):
        halves = [pick(block[:half], index), pick(block[half:], index)]
        return jnp.concatenate(
            [
                jnp.where(first_half, halves[0][r : r + SUB], halves[1][r : r + SUB])
                for r in range(0, half, SUB)
            ],
            axis=0,
        )

    def unpacked(block, index, mask):
        return masked(
            jnp.concatenate([pick(block, index), pick(block, index + layer)], axis=0), mask
        )

    def sent_halo(s, also):
        @pl.when((p < ns - 1) & also)
        def _():
            up_copy(s).wait_send()

        @pl.when((p > 0) & also)
        def _():
            dn_copy(s).wait_send()

    def split(x):
        high = x.astype(jnp.bfloat16)
        low = (x - high.astype(jnp.float32)).astype(jnp.bfloat16)
        return jnp.concatenate([high, high, low, low], axis=0)

    def z_faces(stack):
        product = jnp.dot(f_ref[: 2 * values, :], stack, preferred_element_type=jnp.float32)
        return product[:values], product[values:]

    def send_halo(minus_z, plus_z, s):
        send_up[s] = packed(minus_z, high_index)
        send_dn[s] = packed(plus_z, low_index)

        @pl.when(p < ns - 1)
        def _():
            up_copy(s).start()

        @pl.when(p > 0)
        def _():
            dn_copy(s).start()

    def own_part(b, stack, minus_z, plus_z):
        along_xy = jnp.dot(f_ref[2 * values :, :], stack, preferred_element_type=jnp.float32)
        rest = b - masked(pick(minus_z, own_index[4]), own_mask[4])
        rest = rest - masked(pick(plus_z, own_index[5]), own_mask[5])
        for f in range(4):
            product = along_xy[f * values : (f + 1) * values]
            rest = rest - masked(pick(product, own_index[f]), own_mask[f])
        return rest

    def halo(s):
        @pl.when(p < ns - 1)
        def _():
            dn_copy(s).wait_recv()

        @pl.when(p > 0)
        def _():
            up_copy(s).wait_recv()

        return unpacked(below[s], halo_index[0], halo_mask[0]) + unpacked(
            above[s], halo_index[1], halo_mask[1]
        )

    def send_blocks(c):
        def one(n, carry):
            j = core * (half // 2) + c * chunk + n
            first, second = inv_t[j], inv_t[j + half]
            for dst, index in ((up_blocks, high_index), (dn_blocks, low_index)):
                for r in range(0, values, SUB):
                    dst[j, r : r + SUB, :] = jnp.where(
                        first_half, pick(first[r : r + SUB], index), pick(second[r : r + SUB], index)
                    )
            return carry

        lax.fori_loop(0, chunk, one, 0, unroll=True)

        @pl.when(p < ns - 1)
        def _():
            up_blocks_copy(c).start()

        @pl.when(p > 0)
        def _():
            dn_blocks_copy(c).start()

    def share_blocks(c, also):
        @pl.when((p < ns - 1) & also)
        def _():
            dn_blocks_copy(c).wait_recv()
            hand_on(above_blocks, fd_send, fd_recv, c).start()

        @pl.when((p > 0) & also)
        def _():
            up_blocks_copy(c).wait_recv()
            hand_on(below_blocks, fu_send, fu_recv, c).start()

    def take_blocks():
        for c in range(chunks):

            @pl.when(p < ns - 1)
            def _(c=c):
                up_blocks_copy(c).wait_send()
                hand_on(above_blocks, fd_send, fd_recv, c).wait()

            @pl.when(p > 0)
            def _(c=c):
                dn_blocks_copy(c).wait_send()
                hand_on(below_blocks, fu_send, fu_recv, c).wait()

        def one(j, carry):
            under, over = below_blocks[j], above_blocks[j]
            for at in (0, 1):
                for r in range(0, values, SUB):
                    rows_of = slice(r, r + SUB)
                    over_part = jnp.where(
                        halo_mask[1], pick(over[rows_of], halo_index[1] + at * layer), 0.0
                    )
                    halo_inv_t[j + at * half, rows_of, :] = jnp.where(
                        halo_mask[0], pick(under[rows_of], halo_index[0] + at * layer), over_part
                    )
            return carry

        lax.fori_loop(0, half, one, 0)

    def fine_step(m, field):
        b = field + forcing_ref[m]
        x = apply_inverse(b)
        for sweep in range(SWEEPS):
            stack = split(x)
            minus_z, plus_z = z_faces(stack)
            send_halo(minus_z, plus_z, sweep)
            send_blocks(m * SWEEPS + sweep)
            rest = own_part(b, stack, minus_z, plus_z)
            before = m * SWEEPS + sweep - 1
            share_blocks(jnp.maximum(before, 0), before >= 0)
            rest = rest - halo(sweep)
            if sweep == 0:
                sent_halo(SWEEPS - 1, m > 0)
            else:
                sent_halo(sweep - 1, True)
            x = apply_inverse(rest)
        return x

    def both_sweeps(m, field):
        base = 2 * lax.rem(m + 1, 2)
        b = field + forcing_ref[m]
        x = apply_inverse(b)
        stack = split(x)
        minus_z, plus_z = z_faces(stack)
        send_halo(minus_z, plus_z, base)
        inner = apply_inverse(own_part(b, stack, minus_z, plus_z))
        inner_minus, inner_plus = z_faces(split(inner))
        send_halo(inner_minus, inner_plus, base + 1)
        back = jnp.concatenate(
            [
                jnp.where(halo_mask[0], plus_z[r : r + SUB], minus_z[r : r + SUB])
                for r in range(0, values, SUB)
            ],
            axis=0,
        )
        back_minus, back_plus = z_faces(split(apply_inverse(back, halo_inv_t)))
        back = masked(back_minus, halo_mask[0]) + masked(back_plus, halo_mask[1])
        x = inner - apply_inverse(halo(base))
        stack = split(x)
        minus_z, plus_z = z_faces(stack)
        rest = own_part(b, stack, minus_z, plus_z) + back
        x = apply_inverse(rest - halo(base + 1))
        sent_halo(base, True)
        sent_halo(base + 1, True)
        return x

    def carried_in(first):
        for d in range(1, tm):
            when_scanner(
                lax.rem(k + d, tm), lambda d=d: to_scanner(res, rbuf, d, a_send, a_recv).start()
            )

        if first:
            share_blocks(chunks - 1, True)

        def scan():
            rbuf[k] = res[my_rows, :]
            if first:
                gbuf[k] = gains[my_rows, :]
                for d in range(1, tm):
                    to_scanner(gains, gbuf, d, g_send, g_recv).wait_recv()
            for d in range(1, tm):
                to_scanner(res, rbuf, d, a_send, a_recv).wait_recv()
            running = jnp.zeros((rows, LANES), jnp.float32)
            for lap in range(tm):
                cbuf[lap] = running
                running = gbuf[lap] * running + rbuf[lap]
            for d in range(1, tm):
                from_scanner(d).start()
            cin[my_rows, :] = cbuf[k]

        when_scanner(k, scan)
        if first:
            take_blocks()
        for d in range(1, tm):

            def sent(d=d):
                if first:
                    to_scanner(gains, gbuf, d, g_send, g_recv).wait_send()
                to_scanner(res, rbuf, d, a_send, a_recv).wait_send()

            when_scanner(lax.rem(k + d, tm), sent)
            when_scanner(lax.rem(k + tm - d, tm), lambda d=d: from_scanner(d).wait_recv())

        def returned():
            for d in range(1, tm):
                from_scanner(d).wait_send()

        when_scanner(k, returned)
        return cin[...]

    coarse = jnp.zeros((values, elems), jnp.float32)
    previous = coarse
    for iteration in range(ITERS):
        field = lax.fori_loop(
            0, steps, fine_step if iteration == 0 else both_sweeps, jnp.where(k == 0, init_ref[...], previous)
        )
        if iteration == 0:
            sent_halo(SWEEPS - 1, True)
        residual = field - coarse
        res[...] = residual
        carried = carried_in(iteration == 0)
        previous = previous + carried
        coarse = coarse + (gain_ref[0] * carried + residual)
    out_ref[0] = coarse
    out_ref[1] = residual


def body(tm, ns, initial_state, forcing, coarse_gain, block_inverse, face_blocks, neighbor, send_rows):
    values, elems = initial_state.shape
    steps = forcing.shape[0]
    scanners = min(tm, values // SUB)
    rows = values // scanners
    chunks = SWEEPS * steps
    f32 = jnp.float32
    out = jax.ShapeDtypeStruct((2, values, elems), f32)
    vmem = pl.BlockSpec(memory_space=pltpu.VMEM)
    dma = pltpu.SemaphoreType.DMA
    both = (
        pl.pallas_call(
            functools.partial(kernel, tm, ns, steps),
            out_shape=out,
            in_specs=[pl.BlockSpec(memory_space=pl.ANY)] * 7,
            out_specs=vmem,
            scratch_shapes=[
                pltpu.VMEM((values, elems), f32),
                pltpu.VMEM(forcing.shape, f32),
                pltpu.VMEM((1, values, elems), f32),
                pltpu.VMEM((values * values, elems), f32),
                pltpu.VMEM(face_blocks.shape, f32),
                pltpu.VMEM(neighbor.shape, jnp.int32),
                pltpu.VMEM(send_rows.shape, jnp.int32),
                dma((7,)),
                pltpu.VMEM((values, elems), f32),
                pltpu.VMEM((values, values, elems), f32),
                pltpu.VMEM((values, values, elems), f32),
                pltpu.VMEM((6 * values, 4 * values), f32),
                pltpu.VMEM((6 * values, 4 * values), jnp.bfloat16),
                pltpu.VMEM((values, elems), f32),
                pltpu.VMEM((SUB, elems), jnp.int32),
                pltpu.VMEM((values // 2, values, elems), f32),
                pltpu.VMEM((values // 2, values, elems), f32),
                pltpu.VMEM((values // 2, values, elems), f32),
                pltpu.VMEM((values // 2, values, elems), f32),
                pltpu.VMEM((4, values // 2, elems), f32),
                pltpu.VMEM((4, values // 2, elems), f32),
                pltpu.VMEM((4, values // 2, elems), f32),
                pltpu.VMEM((4, values // 2, elems), f32),
                pltpu.VMEM((tm, rows, elems), f32),
                pltpu.VMEM((tm, rows, elems), f32),
                pltpu.VMEM((tm, rows, elems), f32),
                pltpu.VMEM((values, elems), f32),
                dma((4,)), dma((4,)), dma((4,)), dma((4,)),
                dma((chunks,)), dma((chunks,)), dma((chunks,)), dma((chunks,)),
                dma((chunks,)), dma((chunks,)), dma((chunks,)), dma((chunks,)),
                dma((tm,)), dma((tm,)), dma((tm,)), dma((tm,)), dma((tm,)), dma((tm,)),
            ],
            compiler_params=pltpu.CompilerParams(
                collective_id=0, has_side_effects=True, vmem_limit_bytes=63 * 1024 * 1024
            ),
        )(
            initial_state, forcing, coarse_gain,
            block_inverse.reshape(values * values, elems), face_blocks, neighbor, send_rows,
        )
    )
    return both[:1], both[1:]


def solution(mesh):
    return jax.shard_map(
        functools.partial(body, mesh.shape["tm"], mesh.shape["space"]),
        mesh=mesh,
        in_specs=(
            P(None, "space"),
            P("tm", None, "space"),
            P("tm", None, "space"),
            P(None, None, "space"),
            P(),
            P(None, "space"),
            P(None, "space"),
        ),
        out_specs=(P("tm", None, "space"), P("tm", None, "space")),
        check_vma=False,
    )
```

```python
import functools

import jax
import jax.numpy as jnp
from jax import lax
from jax.experimental import pallas as pl
from jax.experimental.pallas import tpu as pltpu
from jax.sharding import PartitionSpec as P

SWEEPS = 2
ITERS = 2
LANES = 128
SUB = 8
MESH = pl.DeviceIdType.MESH


def pick(block, index):
    return jnp.concatenate(
        [
            jnp.take_along_axis(block[r : r + SUB], index, axis=1, mode="promise_in_bounds")
            for r in range(0, block.shape[0], SUB)
        ],
        axis=0,
    )


def masked(value, mask):
    return jnp.concatenate(
        [jnp.where(mask, value[r : r + SUB], 0.0) for r in range(0, value.shape[0], SUB)], axis=0
    )


def kernel(
    tm, ns, steps,
    init_hbm, forcing_hbm, gain_hbm, inverse_hbm, faces_hbm, neighbor_hbm, send_rows_hbm,
    coarse_ref, residual_ref,
    init_ref, forcing_ref, gain_ref, inverse_ref, faces_ref, neighbor_ref, send_rows_ref,
    load_sem, res,
    inv_t, halo_inv_t, wide, f_ref, r_ref, idx_ref,
    up_blocks, dn_blocks, below_blocks, above_blocks,
    send_up, send_dn, below, above,
    gbuf, rbuf, cbuf, cin,
    up_send, up_recv, dn_send, dn_recv,
    ub_send, ub_recv, db_send, db_recv,
    fu_send, fu_recv, fd_send, fd_recv,
    g_send, g_recv, a_send, a_recv, c_send, c_recv,
):
    values, elems = init_ref.shape
    layer = elems // 2
    half = values // 2
    scanners = min(tm, values // SUB)
    rows = values // scanners
    k = lax.axis_index("tm")
    p = lax.axis_index("space")

    loads = [
        pltpu.make_async_copy(src, dst, load_sem.at[n])
        for n, (src, dst) in enumerate(
            (
                (inverse_hbm, inverse_ref),
                (faces_hbm, faces_ref),
                (neighbor_hbm, neighbor_ref),
                (send_rows_hbm, send_rows_ref),
                (init_hbm, init_ref),
                (forcing_hbm, forcing_ref),
                (gain_hbm, gain_ref),
            )
        )
    ]
    for load in loads:
        load.start()

    barrier = pltpu.get_barrier_semaphore()
    for d in range(1, tm):
        pl.semaphore_signal(barrier, inc=1, device_id=(lax.rem(k + d, tm), p), device_id_type=MESH)

    @pl.when(p > 0)
    def _():
        pl.semaphore_signal(barrier, inc=1, device_id=(k, p - 1), device_id_type=MESH)

    @pl.when(p < ns - 1)
    def _():
        pl.semaphore_signal(barrier, inc=1, device_id=(k, p + 1), device_id_type=MESH)

    for load in loads[1:]:
        load.wait()

    for f in range(6):
        part = faces_ref[(4, 5, 0, 1, 2, 3)[f]]
        high = part.astype(jnp.bfloat16).astype(jnp.float32)
        low = part - high
        for c, piece in enumerate((high, low, high)):
            wide[f * values : (f + 1) * values, c * values : (c + 1) * values] = piece
    f_ref[...] = wide[...].astype(jnp.bfloat16)

    for row in range(2):
        for at in (0, layer):
            idx_ref[row : row + 1, at : at + layer] = send_rows_ref[row : row + 1, :]

    def spread(row):
        return jnp.broadcast_to(row, (SUB, LANES))

    low_index = spread(idx_ref[0:1, :])
    high_index = spread(idx_ref[1:2, :])
    lane = lax.broadcasted_iota(jnp.int32, (SUB, LANES), 1)
    first_half = lane < layer
    side = [spread(neighbor_ref[f : f + 1, :]) for f in range(6)]
    own_mask = [(n >= 0) & (n < elems) for n in side]
    own_index = [jnp.clip(n, 0, elems - 1) for n in side]
    halo_mask, halo_index = [], []
    for n, base in ((side[4], elems), (side[5], elems + layer)):
        halo_mask.append((n >= base) & (n < base + layer))
        halo_index.append(jnp.clip(n - base, 0, layer - 1))

    @pl.when(p == 0)
    def _():
        below[...] = jnp.zeros_like(below)
        below_blocks[...] = jnp.zeros_like(below_blocks)

    @pl.when(p == ns - 1)
    def _():
        above[...] = jnp.zeros_like(above)
        above_blocks[...] = jnp.zeros_like(above_blocks)

    loads[0].wait()

    def turn(j, carry):
        for i in range(0, values, SUB):
            inv_t[j, pl.ds(i, SUB), :] = inverse_ref[pl.ds(i * values + j, SUB, stride=values), :]
        return carry

    lax.fori_loop(0, values, turn, 0, unroll=4)

    expected = tm - 1 + (p > 0).astype(jnp.int32) + (p < ns - 1).astype(jnp.int32)
    pl.semaphore_wait(barrier, expected)

    def when_scanner(place, run):
        if scanners == tm:
            run()
        else:
            pl.when(place < scanners)(run)

    def to_scanner(src, dst, d, send, recv):
        place = lax.rem(k + d, tm)
        return pltpu.make_async_remote_copy(
            src_ref=src.at[pl.ds(pl.multiple_of(lax.rem(place, scanners) * rows, SUB), rows)],
            dst_ref=dst.at[k], send_sem=send.at[d], recv_sem=recv.at[d],
            device_id=(place, p), device_id_type=MESH,
        )

    def from_scanner(d):
        place = lax.rem(k + d, tm)
        return pltpu.make_async_remote_copy(
            src_ref=cbuf.at[place],
            dst_ref=cin.at[pl.ds(pl.multiple_of(lax.rem(k, scanners) * rows, SUB), rows)],
            send_sem=c_send.at[d], recv_sem=c_recv.at[d],
            device_id=(place, p), device_id_type=MESH,
        )

    my_rows = pl.ds(pl.multiple_of(lax.rem(k, scanners) * rows, SUB), rows)
    gains = gain_ref.at[0]
    for d in range(1, tm):
        when_scanner(lax.rem(k + d, tm), lambda d=d: to_scanner(gains, gbuf, d, g_send, g_recv).start())

    def apply_inverse(vector, table=inv_t):
        r_ref[...] = vector
        sums = [None, None]
        for j in range(values):
            term = table[j] * r_ref[j : j + 1, :]
            sums[j % 2] = term if sums[j % 2] is None else sums[j % 2] + term
        return sums[0] + sums[1]

    def up_copy(s):
        return pltpu.make_async_remote_copy(
            src_ref=send_up.at[s], dst_ref=below.at[s], send_sem=up_send.at[s],
            recv_sem=up_recv.at[s], device_id=(k, p + 1), device_id_type=MESH,
        )

    def dn_copy(s):
        return pltpu.make_async_remote_copy(
            src_ref=send_dn.at[s], dst_ref=above.at[s], send_sem=dn_send.at[s],
            recv_sem=dn_recv.at[s], device_id=(k, p - 1), device_id_type=MESH,
        )

    chunks = SWEEPS * steps
    chunk = half // (2 * chunks)
    core = lax.rem(k, 2)
    partner = k + 1 - 2 * core

    def part_of(c):
        return pl.ds(core * (half // 2) + c * chunk, chunk)

    def hand_on(blocks, send, recv, c):
        part = part_of(c)
        return pltpu.make_async_remote_copy(
            src_ref=blocks.at[part], dst_ref=blocks.at[part], send_sem=send.at[c],
            recv_sem=recv.at[c], device_id=(partner, p), device_id_type=MESH,
        )

    def up_blocks_copy(c):
        part = part_of(c)
        return pltpu.make_async_remote_copy(
            src_ref=up_blocks.at[part], dst_ref=below_blocks.at[part], send_sem=ub_send.at[c],
            recv_sem=ub_recv.at[c], device_id=(k, p + 1), device_id_type=MESH,
        )

    def dn_blocks_copy(c):
        part = part_of(c)
        return pltpu.make_async_remote_copy(
            src_ref=dn_blocks.at[part], dst_ref=above_blocks.at[part], send_sem=db_send.at[c],
            recv_sem=db_recv.at[c], device_id=(k, p - 1), device_id_type=MESH,
        )

    def packed(block, index):
        halves = [pick(block[:half], index), pick(block[half:], index)]
        return jnp.concatenate(
            [
                jnp.where(first_half, halves[0][r : r + SUB], halves[1][r : r + SUB])
                for r in range(0, half, SUB)
            ],
            axis=0,
        )

    def unpacked(block, index, mask):
        return masked(
            jnp.concatenate([pick(block, index), pick(block, index + layer)], axis=0), mask
        )

    def sent_halo(s, also):
        @pl.when((p < ns - 1) & also)
        def _():
            up_copy(s).wait_send()

        @pl.when((p > 0) & also)
        def _():
            dn_copy(s).wait_send()

    def split(x):
        high = x.astype(jnp.bfloat16)
        low = (x - high.astype(jnp.float32)).astype(jnp.bfloat16)
        return jnp.concatenate([high, high, low], axis=0)

    def z_faces(stack):
        product = jnp.dot(f_ref[: 2 * values, :], stack, preferred_element_type=jnp.float32)
        return product[:values], product[values:]

    def send_halo(minus_z, plus_z, s):
        send_up[s] = packed(minus_z, high_index)
        send_dn[s] = packed(plus_z, low_index)

        @pl.when(p < ns - 1)
        def _():
            up_copy(s).start()

        @pl.when(p > 0)
        def _():
            dn_copy(s).start()

    def own_part(b, stack, minus_z, plus_z):
        along_xy = jnp.dot(f_ref[2 * values :, :], stack, preferred_element_type=jnp.float32)
        rest = b - masked(pick(minus_z, own_index[4]), own_mask[4])
        rest = rest - masked(pick(plus_z, own_index[5]), own_mask[5])
        for f in range(4):
            product = along_xy[f * values : (f + 1) * values]
            rest = rest - masked(pick(product, own_index[f]), own_mask[f])
        return rest

    def halo(s):
        @pl.when(p < ns - 1)
        def _():
            dn_copy(s).wait_recv()

        @pl.when(p > 0)
        def _():
            up_copy(s).wait_recv()

        return unpacked(below[s], halo_index[0], halo_mask[0]) + unpacked(
            above[s], halo_index[1], halo_mask[1]
        )

    def send_blocks(c):
        def one(n, carry):
            j = core * (half // 2) + c * chunk + n
            first, second = inv_t[j], inv_t[j + half]
            for dst, index in ((up_blocks, high_index), (dn_blocks, low_index)):
                for r in range(0, values, SUB):
                    dst[j, r : r + SUB, :] = jnp.where(
                        first_half, pick(first[r : r + SUB], index), pick(second[r : r + SUB], index)
                    )
            return carry

        lax.fori_loop(0, chunk, one, 0, unroll=True)

        @pl.when(p < ns - 1)
        def _():
            up_blocks_copy(c).start()

        @pl.when(p > 0)
        def _():
            dn_blocks_copy(c).start()

    def share_blocks(c, also):
        @pl.when((p < ns - 1) & also)
        def _():
            dn_blocks_copy(c).wait_recv()
            hand_on(above_blocks, fd_send, fd_recv, c).start()

        @pl.when((p > 0) & also)
        def _():
            up_blocks_copy(c).wait_recv()
            hand_on(below_blocks, fu_send, fu_recv, c).start()

    def take_blocks():
        for c in range(chunks):

            @pl.when(p < ns - 1)
            def _(c=c):
                up_blocks_copy(c).wait_send()
                hand_on(above_blocks, fd_send, fd_recv, c).wait()

            @pl.when(p > 0)
            def _(c=c):
                dn_blocks_copy(c).wait_send()
                hand_on(below_blocks, fu_send, fu_recv, c).wait()

        def one(j, carry):
            under, over = below_blocks[j], above_blocks[j]
            for at in (0, 1):
                for r in range(0, values, SUB):
                    rows_of = slice(r, r + SUB)
                    over_part = jnp.where(
                        halo_mask[1], pick(over[rows_of], halo_index[1] + at * layer), 0.0
                    )
                    halo_inv_t[j + at * half, rows_of, :] = jnp.where(
                        halo_mask[0], pick(under[rows_of], halo_index[0] + at * layer), over_part
                    )
            return carry

        lax.fori_loop(0, half, one, 0, unroll=8)

    def fine_step(m, field):
        b = field + forcing_ref[m]
        x = apply_inverse(b)
        for sweep in range(SWEEPS):
            stack = split(x)
            minus_z, plus_z = z_faces(stack)
            send_halo(minus_z, plus_z, sweep)
            send_blocks(m * SWEEPS + sweep)
            rest = own_part(b, stack, minus_z, plus_z)
            before = m * SWEEPS + sweep - 1
            share_blocks(jnp.maximum(before, 0), before >= 0)
            rest = rest - halo(sweep)
            if sweep == 0:
                sent_halo(SWEEPS - 1, m > 0)
            else:
                sent_halo(sweep - 1, True)
            x = apply_inverse(rest)
        return x

    def both_sweeps(m, field):
        base = 2 * lax.rem(m + 1, 2)
        b = field + forcing_ref[m]
        x = apply_inverse(b)
        stack = split(x)
        minus_z, plus_z = z_faces(stack)
        send_halo(minus_z, plus_z, base)
        inner = apply_inverse(own_part(b, stack, minus_z, plus_z))
        inner_minus, inner_plus = z_faces(split(inner))
        send_halo(inner_minus, inner_plus, base + 1)
        back = jnp.concatenate(
            [
                jnp.where(halo_mask[0], plus_z[r : r + SUB], minus_z[r : r + SUB])
                for r in range(0, values, SUB)
            ],
            axis=0,
        )
        back_minus, back_plus = z_faces(split(apply_inverse(back, halo_inv_t)))
        back = masked(back_minus, halo_mask[0]) + masked(back_plus, halo_mask[1])
        x = inner - apply_inverse(halo(base))
        stack = split(x)
        minus_z, plus_z = z_faces(stack)
        rest = own_part(b, stack, minus_z, plus_z) + back
        x = apply_inverse(rest - halo(base + 1))
        sent_halo(base, True)
        sent_halo(base + 1, True)
        return x

    def carried_in(first):
        for d in range(1, tm):
            when_scanner(
                lax.rem(k + d, tm), lambda d=d: to_scanner(res, rbuf, d, a_send, a_recv).start()
            )

        if first:
            share_blocks(chunks - 1, True)

        def scan():
            rbuf[k] = res[my_rows, :]
            if first:
                gbuf[k] = gains[my_rows, :]
                for d in range(1, tm):
                    to_scanner(gains, gbuf, d, g_send, g_recv).wait_recv()
            for d in range(1, tm):
                to_scanner(res, rbuf, d, a_send, a_recv).wait_recv()
            running = jnp.zeros((rows, LANES), jnp.float32)
            for lap in range(tm):
                cbuf[lap] = running
                running = gbuf[lap] * running + rbuf[lap]
            for d in range(1, tm):
                from_scanner(d).start()
            cin[my_rows, :] = cbuf[k]

        when_scanner(k, scan)
        if first:
            take_blocks()
        for d in range(1, tm):

            def sent(d=d):
                if first:
                    to_scanner(gains, gbuf, d, g_send, g_recv).wait_send()
                to_scanner(res, rbuf, d, a_send, a_recv).wait_send()

            when_scanner(lax.rem(k + d, tm), sent)
            when_scanner(lax.rem(k + tm - d, tm), lambda d=d: from_scanner(d).wait_recv())

        def returned():
            for d in range(1, tm):
                from_scanner(d).wait_send()

        when_scanner(k, returned)
        return cin[...]

    coarse = jnp.zeros((values, elems), jnp.float32)
    previous = coarse
    for iteration in range(ITERS):
        field = lax.fori_loop(
            0, steps, fine_step if iteration == 0 else both_sweeps, jnp.where(k == 0, init_ref[...], previous)
        )
        if iteration == 0:
            sent_halo(SWEEPS - 1, True)
        residual = field - coarse
        res[...] = residual
        carried = carried_in(iteration == 0)
        previous = previous + carried
        coarse = coarse + (gain_ref[0] * carried + residual)
    coarse_ref[0] = coarse
    residual_ref[0] = residual


def body(tm, ns, initial_state, forcing, coarse_gain, block_inverse, face_blocks, neighbor, send_rows):
    values, elems = initial_state.shape
    steps = forcing.shape[0]
    scanners = min(tm, values // SUB)
    rows = values // scanners
    chunks = SWEEPS * steps
    f32 = jnp.float32
    out = jax.ShapeDtypeStruct((1, values, elems), f32)
    vmem = pl.BlockSpec(memory_space=pltpu.VMEM)
    dma = pltpu.SemaphoreType.DMA
    return tuple(
        pl.pallas_call(
            functools.partial(kernel, tm, ns, steps),
            out_shape=(out, out),
            in_specs=[pl.BlockSpec(memory_space=pl.ANY)] * 7,
            out_specs=(vmem, vmem),
            scratch_shapes=[
                pltpu.VMEM((values, elems), f32),
                pltpu.VMEM(forcing.shape, f32),
                pltpu.VMEM((1, values, elems), f32),
                pltpu.VMEM((values * values, elems), f32),
                pltpu.VMEM(face_blocks.shape, f32),
                pltpu.VMEM(neighbor.shape, jnp.int32),
                pltpu.VMEM(send_rows.shape, jnp.int32),
                dma((7,)),
                pltpu.VMEM((values, elems), f32),
                pltpu.VMEM((values, values, elems), f32),
                pltpu.VMEM((values, values, elems), f32),
                pltpu.VMEM((6 * values, 3 * values), f32),
                pltpu.VMEM((6 * values, 3 * values), jnp.bfloat16),
                pltpu.VMEM((values, elems), f32),
                pltpu.VMEM((SUB, elems), jnp.int32),
                pltpu.VMEM((values // 2, values, elems), f32),
                pltpu.VMEM((values // 2, values, elems), f32),
                pltpu.VMEM((values // 2, values, elems), f32),
                pltpu.VMEM((values // 2, values, elems), f32),
                pltpu.VMEM((4, values // 2, elems), f32),
                pltpu.VMEM((4, values // 2, elems), f32),
                pltpu.VMEM((4, values // 2, elems), f32),
                pltpu.VMEM((4, values // 2, elems), f32),
                pltpu.VMEM((tm, rows, elems), f32),
                pltpu.VMEM((tm, rows, elems), f32),
                pltpu.VMEM((tm, rows, elems), f32),
                pltpu.VMEM((values, elems), f32),
                dma((4,)), dma((4,)), dma((4,)), dma((4,)),
                dma((chunks,)), dma((chunks,)), dma((chunks,)), dma((chunks,)),
                dma((chunks,)), dma((chunks,)), dma((chunks,)), dma((chunks,)),
                dma((tm,)), dma((tm,)), dma((tm,)), dma((tm,)), dma((tm,)), dma((tm,)),
            ],
            compiler_params=pltpu.CompilerParams(
                collective_id=0, has_side_effects=True, vmem_limit_bytes=63 * 1024 * 1024
            ),
        )(
            initial_state, forcing, coarse_gain,
            block_inverse.reshape(values * values, elems), face_blocks, neighbor, send_rows,
        )
    )


def solution(mesh):
    return jax.shard_map(
        functools.partial(body, mesh.shape["tm"], mesh.shape["space"]),
        mesh=mesh,
        in_specs=(
            P(None, "space"),
            P("tm", None, "space"),
            P("tm", None, "space"),
            P(None, None, "space"),
            P(),
            P(None, "space"),
            P(None, "space"),
        ),
        out_specs=(P("tm", None, "space"), P("tm", None, "space")),
        check_vma=False,
    )
```

```python
import functools

import jax
import jax.numpy as jnp
from jax import lax
from jax.experimental import pallas as pl
from jax.experimental.pallas import tpu as pltpu
from jax.sharding import PartitionSpec as P

SWEEPS = 2
ITERS = 2
LANES = 128
SUB = 8
MESH = pl.DeviceIdType.MESH


def pick(block, index):
    return jnp.concatenate(
        [
            jnp.take_along_axis(block[r : r + SUB], index, axis=1, mode="promise_in_bounds")
            for r in range(0, block.shape[0], SUB)
        ],
        axis=0,
    )


def masked(value, mask):
    return jnp.concatenate(
        [jnp.where(mask, value[r : r + SUB], 0.0) for r in range(0, value.shape[0], SUB)], axis=0
    )


def kernel(
    tm, ns, steps,
    init_hbm, forcing_hbm, gain_hbm, inverse_hbm, faces_hbm, neighbor_hbm, send_rows_hbm,
    out_ref,
    init_ref, forcing_ref, gain_ref, inverse_ref, faces_ref, neighbor_ref, send_rows_ref,
    load_sem, res,
    inv_t, halo_inv_t, wide, f_ref, r_ref, idx_ref,
    up_blocks, dn_blocks, below_blocks, above_blocks,
    send_up, send_dn, below, above,
    gbuf, rbuf, cbuf, cin,
    up_send, up_recv, dn_send, dn_recv,
    ub_send, ub_recv, db_send, db_recv,
    fu_send, fu_recv, fd_send, fd_recv,
    g_send, g_recv, a_send, a_recv, c_send, c_recv,
):
    values, elems = init_ref.shape
    layer = elems // 2
    half = values // 2
    scanners = min(tm, values // SUB)
    rows = values // scanners
    k = lax.axis_index("tm")
    p = lax.axis_index("space")

    loads = [
        pltpu.make_async_copy(src, dst, load_sem.at[n])
        for n, (src, dst) in enumerate(
            (
                (inverse_hbm, inverse_ref),
                (faces_hbm, faces_ref),
                (neighbor_hbm, neighbor_ref),
                (send_rows_hbm, send_rows_ref),
                (init_hbm, init_ref),
                (forcing_hbm, forcing_ref),
                (gain_hbm, gain_ref),
            )
        )
    ]
    for load in loads:
        load.start()

    barrier = pltpu.get_barrier_semaphore()
    for d in range(1, tm):
        pl.semaphore_signal(barrier, inc=1, device_id=(lax.rem(k + d, tm), p), device_id_type=MESH)

    @pl.when(p > 0)
    def _():
        pl.semaphore_signal(barrier, inc=1, device_id=(k, p - 1), device_id_type=MESH)

    @pl.when(p < ns - 1)
    def _():
        pl.semaphore_signal(barrier, inc=1, device_id=(k, p + 1), device_id_type=MESH)

    for load in loads[1:]:
        load.wait()

    for f in range(6):
        part = faces_ref[(4, 5, 0, 1, 2, 3)[f]]
        high = part.astype(jnp.bfloat16).astype(jnp.float32)
        low = part - high
        for c, piece in enumerate((high, low, high)):
            wide[f * values : (f + 1) * values, c * values : (c + 1) * values] = piece
    f_ref[...] = wide[...].astype(jnp.bfloat16)

    for row in range(2):
        for at in (0, layer):
            idx_ref[row : row + 1, at : at + layer] = send_rows_ref[row : row + 1, :]

    def spread(row):
        return jnp.broadcast_to(row, (SUB, LANES))

    low_index = spread(idx_ref[0:1, :])
    high_index = spread(idx_ref[1:2, :])
    lane = lax.broadcasted_iota(jnp.int32, (SUB, LANES), 1)
    first_half = lane < layer
    side = [spread(neighbor_ref[f : f + 1, :]) for f in range(6)]
    own_mask = [(n >= 0) & (n < elems) for n in side]
    own_index = [jnp.clip(n, 0, elems - 1) for n in side]
    halo_mask, halo_index = [], []
    for n, base in ((side[4], elems), (side[5], elems + layer)):
        halo_mask.append((n >= base) & (n < base + layer))
        halo_index.append(jnp.clip(n - base, 0, layer - 1))

    @pl.when(p == 0)
    def _():
        below[...] = jnp.zeros_like(below)
        below_blocks[...] = jnp.zeros_like(below_blocks)

    @pl.when(p == ns - 1)
    def _():
        above[...] = jnp.zeros_like(above)
        above_blocks[...] = jnp.zeros_like(above_blocks)

    loads[0].wait()

    def turn(j, carry):
        for i in range(0, values, SUB):
            inv_t[j, pl.ds(i, SUB), :] = inverse_ref[pl.ds(i * values + j, SUB, stride=values), :]
        return carry

    lax.fori_loop(0, values, turn, 0, unroll=8)

    expected = tm - 1 + (p > 0).astype(jnp.int32) + (p < ns - 1).astype(jnp.int32)
    pl.semaphore_wait(barrier, expected)

    def when_scanner(place, run):
        if scanners == tm:
            run()
        else:
            pl.when(place < scanners)(run)

    def to_scanner(src, dst, d, send, recv):
        place = lax.rem(k + d, tm)
        return pltpu.make_async_remote_copy(
            src_ref=src.at[pl.ds(pl.multiple_of(lax.rem(place, scanners) * rows, SUB), rows)],
            dst_ref=dst.at[k], send_sem=send.at[d], recv_sem=recv.at[d],
            device_id=(place, p), device_id_type=MESH,
        )

    def from_scanner(d):
        place = lax.rem(k + d, tm)
        return pltpu.make_async_remote_copy(
            src_ref=cbuf.at[place],
            dst_ref=cin.at[pl.ds(pl.multiple_of(lax.rem(k, scanners) * rows, SUB), rows)],
            send_sem=c_send.at[d], recv_sem=c_recv.at[d],
            device_id=(place, p), device_id_type=MESH,
        )

    my_rows = pl.ds(pl.multiple_of(lax.rem(k, scanners) * rows, SUB), rows)
    gains = gain_ref.at[0]
    for d in range(1, tm):
        when_scanner(lax.rem(k + d, tm), lambda d=d: to_scanner(gains, gbuf, d, g_send, g_recv).start())

    def apply_inverse(vector, table=inv_t):
        r_ref[...] = vector
        sums = [None, None]
        for j in range(values):
            term = table[j] * r_ref[j : j + 1, :]
            sums[j % 2] = term if sums[j % 2] is None else sums[j % 2] + term
        return sums[0] + sums[1]

    def up_copy(s):
        return pltpu.make_async_remote_copy(
            src_ref=send_up.at[s], dst_ref=below.at[s], send_sem=up_send.at[s],
            recv_sem=up_recv.at[s], device_id=(k, p + 1), device_id_type=MESH,
        )

    def dn_copy(s):
        return pltpu.make_async_remote_copy(
            src_ref=send_dn.at[s], dst_ref=above.at[s], send_sem=dn_send.at[s],
            recv_sem=dn_recv.at[s], device_id=(k, p - 1), device_id_type=MESH,
        )

    chunks = SWEEPS * steps
    chunk = half // (2 * chunks)
    core = lax.rem(k, 2)
    partner = k + 1 - 2 * core

    def part_of(c):
        return pl.ds(core * (half // 2) + c * chunk, chunk)

    def hand_on(blocks, send, recv, c):
        part = part_of(c)
        return pltpu.make_async_remote_copy(
            src_ref=blocks.at[part], dst_ref=blocks.at[part], send_sem=send.at[c],
            recv_sem=recv.at[c], device_id=(partner, p), device_id_type=MESH,
        )

    def up_blocks_copy(c):
        part = part_of(c)
        return pltpu.make_async_remote_copy(
            src_ref=up_blocks.at[part], dst_ref=below_blocks.at[part], send_sem=ub_send.at[c],
            recv_sem=ub_recv.at[c], device_id=(k, p + 1), device_id_type=MESH,
        )

    def dn_blocks_copy(c):
        part = part_of(c)
        return pltpu.make_async_remote_copy(
            src_ref=dn_blocks.at[part], dst_ref=above_blocks.at[part], send_sem=db_send.at[c],
            recv_sem=db_recv.at[c], device_id=(k, p - 1), device_id_type=MESH,
        )

    def packed(block, index):
        halves = [pick(block[:half], index), pick(block[half:], index)]
        return jnp.concatenate(
            [
                jnp.where(first_half, halves[0][r : r + SUB], halves[1][r : r + SUB])
                for r in range(0, half, SUB)
            ],
            axis=0,
        )

    def unpacked(block, index, mask):
        return masked(
            jnp.concatenate([pick(block, index), pick(block, index + layer)], axis=0), mask
        )

    def sent_halo(s, also):
        @pl.when((p < ns - 1) & also)
        def _():
            up_copy(s).wait_send()

        @pl.when((p > 0) & also)
        def _():
            dn_copy(s).wait_send()

    def split(x):
        high = x.astype(jnp.bfloat16)
        low = (x - high.astype(jnp.float32)).astype(jnp.bfloat16)
        return jnp.concatenate([high, high, low], axis=0)

    def z_faces(stack):
        product = jnp.dot(f_ref[: 2 * values, :], stack, preferred_element_type=jnp.float32)
        return product[:values], product[values:]

    def send_halo(minus_z, plus_z, s):
        send_up[s] = packed(minus_z, high_index)
        send_dn[s] = packed(plus_z, low_index)

        @pl.when(p < ns - 1)
        def _():
            up_copy(s).start()

        @pl.when(p > 0)
        def _():
            dn_copy(s).start()

    def own_part(b, stack, minus_z, plus_z):
        along_xy = jnp.dot(f_ref[2 * values :, :], stack, preferred_element_type=jnp.float32)
        rest = b - masked(pick(minus_z, own_index[4]), own_mask[4])
        rest = rest - masked(pick(plus_z, own_index[5]), own_mask[5])
        for f in range(4):
            product = along_xy[f * values : (f + 1) * values]
            rest = rest - masked(pick(product, own_index[f]), own_mask[f])
        return rest

    def halo(s):
        @pl.when(p < ns - 1)
        def _():
            dn_copy(s).wait_recv()

        @pl.when(p > 0)
        def _():
            up_copy(s).wait_recv()

        return unpacked(below[s], halo_index[0], halo_mask[0]) + unpacked(
            above[s], halo_index[1], halo_mask[1]
        )

    def send_blocks(c):
        def one(n, carry):
            j = core * (half // 2) + c * chunk + n
            first, second = inv_t[j], inv_t[j + half]
            for dst, index in ((up_blocks, high_index), (dn_blocks, low_index)):
                for r in range(0, values, SUB):
                    dst[j, r : r + SUB, :] = jnp.where(
                        first_half, pick(first[r : r + SUB], index), pick(second[r : r + SUB], index)
                    )
            return carry

        lax.fori_loop(0, chunk, one, 0, unroll=True)

        @pl.when(p < ns - 1)
        def _():
            up_blocks_copy(c).start()

        @pl.when(p > 0)
        def _():
            dn_blocks_copy(c).start()

    def share_blocks(c, also):
        @pl.when((p < ns - 1) & also)
        def _():
            dn_blocks_copy(c).wait_recv()
            hand_on(above_blocks, fd_send, fd_recv, c).start()

        @pl.when((p > 0) & also)
        def _():
            up_blocks_copy(c).wait_recv()
            hand_on(below_blocks, fu_send, fu_recv, c).start()

    def take_blocks():
        for c in range(chunks):

            @pl.when(p < ns - 1)
            def _(c=c):
                up_blocks_copy(c).wait_send()
                hand_on(above_blocks, fd_send, fd_recv, c).wait()

            @pl.when(p > 0)
            def _(c=c):
                dn_blocks_copy(c).wait_send()
                hand_on(below_blocks, fu_send, fu_recv, c).wait()

        def one(j, carry):
            under, over = below_blocks[j], above_blocks[j]
            for at in (0, 1):
                for r in range(0, values, SUB):
                    rows_of = slice(r, r + SUB)
                    over_part = jnp.where(
                        halo_mask[1], pick(over[rows_of], halo_index[1] + at * layer), 0.0
                    )
                    halo_inv_t[j + at * half, rows_of, :] = jnp.where(
                        halo_mask[0], pick(under[rows_of], halo_index[0] + at * layer), over_part
                    )
            return carry

        lax.fori_loop(0, half, one, 0, unroll=8)

    def fine_step(m, field):
        b = field + forcing_ref[m]
        x = apply_inverse(b)
        for sweep in range(SWEEPS):
            stack = split(x)
            minus_z, plus_z = z_faces(stack)
            send_halo(minus_z, plus_z, sweep)
            send_blocks(m * SWEEPS + sweep)
            rest = own_part(b, stack, minus_z, plus_z)
            before = m * SWEEPS + sweep - 1
            share_blocks(jnp.maximum(before, 0), before >= 0)
            rest = rest - halo(sweep)
            if sweep == 0:
                sent_halo(SWEEPS - 1, m > 0)
            else:
                sent_halo(sweep - 1, True)
            x = apply_inverse(rest)
        return x

    def both_sweeps(m, field):
        base = 2 * lax.rem(m + 1, 2)
        b = field + forcing_ref[m]
        x = apply_inverse(b)
        stack = split(x)
        minus_z, plus_z = z_faces(stack)
        send_halo(minus_z, plus_z, base)
        inner = apply_inverse(own_part(b, stack, minus_z, plus_z))
        inner_minus, inner_plus = z_faces(split(inner))
        send_halo(inner_minus, inner_plus, base + 1)
        back = jnp.concatenate(
            [
                jnp.where(halo_mask[0], plus_z[r : r + SUB], minus_z[r : r + SUB])
                for r in range(0, values, SUB)
            ],
            axis=0,
        )
        back_minus, back_plus = z_faces(split(apply_inverse(back, halo_inv_t)))
        back = masked(back_minus, halo_mask[0]) + masked(back_plus, halo_mask[1])
        x = inner - apply_inverse(halo(base))
        stack = split(x)
        minus_z, plus_z = z_faces(stack)
        rest = own_part(b, stack, minus_z, plus_z) + back
        x = apply_inverse(rest - halo(base + 1))
        sent_halo(base, True)
        sent_halo(base + 1, True)
        return x

    def carried_in(first):
        for d in range(1, tm):
            when_scanner(
                lax.rem(k + d, tm), lambda d=d: to_scanner(res, rbuf, d, a_send, a_recv).start()
            )

        if first:
            share_blocks(chunks - 1, True)

        def scan():
            rbuf[k] = res[my_rows, :]
            if first:
                gbuf[k] = gains[my_rows, :]
                for d in range(1, tm):
                    to_scanner(gains, gbuf, d, g_send, g_recv).wait_recv()
            for d in range(1, tm):
                to_scanner(res, rbuf, d, a_send, a_recv).wait_recv()
            running = jnp.zeros((rows, LANES), jnp.float32)
            for lap in range(tm):
                cbuf[lap] = running
                running = gbuf[lap] * running + rbuf[lap]
            for d in range(1, tm):
                from_scanner(d).start()
            cin[my_rows, :] = cbuf[k]

        when_scanner(k, scan)
        if first:
            take_blocks()
        for d in range(1, tm):

            def sent(d=d):
                if first:
                    to_scanner(gains, gbuf, d, g_send, g_recv).wait_send()
                to_scanner(res, rbuf, d, a_send, a_recv).wait_send()

            when_scanner(lax.rem(k + d, tm), sent)
            when_scanner(lax.rem(k + tm - d, tm), lambda d=d: from_scanner(d).wait_recv())

        def returned():
            for d in range(1, tm):
                from_scanner(d).wait_send()

        when_scanner(k, returned)
        return cin[...]

    coarse = jnp.zeros((values, elems), jnp.float32)
    previous = coarse
    for iteration in range(ITERS):
        field = lax.fori_loop(
            0, steps, fine_step if iteration == 0 else both_sweeps, jnp.where(k == 0, init_ref[...], previous)
        )
        if iteration == 0:
            sent_halo(SWEEPS - 1, True)
        residual = field - coarse
        res[...] = residual
        carried = carried_in(iteration == 0)
        previous = previous + carried
        coarse = coarse + (gain_ref[0] * carried + residual)
    out_ref[0] = coarse
    out_ref[1] = residual


def body(tm, ns, initial_state, forcing, coarse_gain, block_inverse, face_blocks, neighbor, send_rows):
    values, elems = initial_state.shape
    steps = forcing.shape[0]
    scanners = min(tm, values // SUB)
    rows = values // scanners
    chunks = SWEEPS * steps
    f32 = jnp.float32
    out = jax.ShapeDtypeStruct((2, values, elems), f32)
    vmem = pl.BlockSpec(memory_space=pltpu.VMEM)
    dma = pltpu.SemaphoreType.DMA
    both = (
        pl.pallas_call(
            functools.partial(kernel, tm, ns, steps),
            out_shape=out,
            in_specs=[pl.BlockSpec(memory_space=pl.ANY)] * 7,
            out_specs=vmem,
            scratch_shapes=[
                pltpu.VMEM((values, elems), f32),
                pltpu.VMEM(forcing.shape, f32),
                pltpu.VMEM((1, values, elems), f32),
                pltpu.VMEM((values * values, elems), f32),
                pltpu.VMEM(face_blocks.shape, f32),
                pltpu.VMEM(neighbor.shape, jnp.int32),
                pltpu.VMEM(send_rows.shape, jnp.int32),
                dma((7,)),
                pltpu.VMEM((values, elems), f32),
                pltpu.VMEM((values, values, elems), f32),
                pltpu.VMEM((values, values, elems), f32),
                pltpu.VMEM((6 * values, 3 * values), f32),
                pltpu.VMEM((6 * values, 3 * values), jnp.bfloat16),
                pltpu.VMEM((values, elems), f32),
                pltpu.VMEM((SUB, elems), jnp.int32),
                pltpu.VMEM((values // 2, values, elems), f32),
                pltpu.VMEM((values // 2, values, elems), f32),
                pltpu.VMEM((values // 2, values, elems), f32),
                pltpu.VMEM((values // 2, values, elems), f32),
                pltpu.VMEM((4, values // 2, elems), f32),
                pltpu.VMEM((4, values // 2, elems), f32),
                pltpu.VMEM((4, values // 2, elems), f32),
                pltpu.VMEM((4, values // 2, elems), f32),
                pltpu.VMEM((tm, rows, elems), f32),
                pltpu.VMEM((tm, rows, elems), f32),
                pltpu.VMEM((tm, rows, elems), f32),
                pltpu.VMEM((values, elems), f32),
                dma((4,)), dma((4,)), dma((4,)), dma((4,)),
                dma((chunks,)), dma((chunks,)), dma((chunks,)), dma((chunks,)),
                dma((chunks,)), dma((chunks,)), dma((chunks,)), dma((chunks,)),
                dma((tm,)), dma((tm,)), dma((tm,)), dma((tm,)), dma((tm,)), dma((tm,)),
            ],
            compiler_params=pltpu.CompilerParams(
                collective_id=0, has_side_effects=True, vmem_limit_bytes=63 * 1024 * 1024
            ),
        )(
            initial_state, forcing, coarse_gain,
            block_inverse.reshape(values * values, elems), face_blocks, neighbor, send_rows,
        )
    )
    return both[:1], both[1:]


def solution(mesh):
    return jax.shard_map(
        functools.partial(body, mesh.shape["tm"], mesh.shape["space"]),
        mesh=mesh,
        in_specs=(
            P(None, "space"),
            P("tm", None, "space"),
            P("tm", None, "space"),
            P(None, None, "space"),
            P(),
            P(None, "space"),
            P(None, "space"),
        ),
        out_specs=(P("tm", None, "space"), P("tm", None, "space")),
        check_vma=False,
    )
```

```python
import functools

import jax
import jax.numpy as jnp
from jax import lax
from jax.experimental import pallas as pl
from jax.experimental.pallas import tpu as pltpu
from jax.sharding import PartitionSpec as P

SWEEPS = 2
ITERS = 2
LANES = 128
SUB = 8
MESH = pl.DeviceIdType.MESH


def pick(block, index):
    return jnp.concatenate(
        [
            jnp.take_along_axis(block[r : r + SUB], index, axis=1, mode="promise_in_bounds")
            for r in range(0, block.shape[0], SUB)
        ],
        axis=0,
    )


def masked(value, mask):
    return jnp.concatenate(
        [jnp.where(mask, value[r : r + SUB], 0.0) for r in range(0, value.shape[0], SUB)], axis=0
    )


def kernel(
    tm, ns, steps,
    init_hbm, forcing_hbm, gain_hbm, inverse_hbm, faces_hbm, neighbor_hbm, send_rows_hbm,
    out_ref,
    init_ref, forcing_ref, gain_ref, inverse_ref, faces_ref, neighbor_ref, send_rows_ref,
    load_sem, res,
    inv_t, halo_inv_t, wide, f_ref, r_ref, idx_ref,
    up_blocks, dn_blocks, below_blocks, above_blocks,
    send_up, send_dn, below, above,
    gbuf, rbuf, cbuf, cin,
    up_send, up_recv, dn_send, dn_recv,
    ub_send, ub_recv, db_send, db_recv,
    fu_send, fu_recv, fd_send, fd_recv,
    g_send, g_recv, a_send, a_recv, c_send, c_recv,
):
    values, elems = init_ref.shape
    layer = elems // 2
    half = values // 2
    scanners = min(tm, values // SUB)
    rows = values // scanners
    k = lax.axis_index("tm")
    p = lax.axis_index("space")

    loads = [
        pltpu.make_async_copy(src, dst, load_sem.at[n])
        for n, (src, dst) in enumerate(
            (
                (inverse_hbm, inverse_ref),
                (faces_hbm, faces_ref),
                (neighbor_hbm, neighbor_ref),
                (send_rows_hbm, send_rows_ref),
                (init_hbm, init_ref),
                (forcing_hbm, forcing_ref),
                (gain_hbm, gain_ref),
            )
        )
    ]
    for load in loads:
        load.start()

    barrier = pltpu.get_barrier_semaphore()
    for d in range(1, tm):
        pl.semaphore_signal(barrier, inc=1, device_id=(lax.rem(k + d, tm), p), device_id_type=MESH)

    @pl.when(p > 0)
    def _():
        pl.semaphore_signal(barrier, inc=1, device_id=(k, p - 1), device_id_type=MESH)

    @pl.when(p < ns - 1)
    def _():
        pl.semaphore_signal(barrier, inc=1, device_id=(k, p + 1), device_id_type=MESH)

    for load in loads[1:]:
        load.wait()

    for f in range(6):
        part = faces_ref[(4, 5, 0, 1, 2, 3)[f]]
        high = part.astype(jnp.bfloat16).astype(jnp.float32)
        low = part - high
        for c, piece in enumerate((high, low, high)):
            wide[f * values : (f + 1) * values, c * values : (c + 1) * values] = piece
    f_ref[...] = wide[...].astype(jnp.bfloat16)

    for row in range(2):
        for at in (0, layer):
            idx_ref[row : row + 1, at : at + layer] = send_rows_ref[row : row + 1, :]

    def spread(row):
        return jnp.broadcast_to(row, (SUB, LANES))

    low_index = spread(idx_ref[0:1, :])
    high_index = spread(idx_ref[1:2, :])
    lane = lax.broadcasted_iota(jnp.int32, (SUB, LANES), 1)
    first_half = lane < layer
    side = [spread(neighbor_ref[f : f + 1, :]) for f in range(6)]
    own_mask = [(n >= 0) & (n < elems) for n in side]
    own_index = [jnp.clip(n, 0, elems - 1) for n in side]
    halo_mask, halo_index = [], []
    for n, base in ((side[4], elems), (side[5], elems + layer)):
        halo_mask.append((n >= base) & (n < base + layer))
        halo_index.append(jnp.clip(n - base, 0, layer - 1))

    @pl.when(p == 0)
    def _():
        below[...] = jnp.zeros_like(below)
        below_blocks[...] = jnp.zeros_like(below_blocks)

    @pl.when(p == ns - 1)
    def _():
        above[...] = jnp.zeros_like(above)
        above_blocks[...] = jnp.zeros_like(above_blocks)

    loads[0].wait()

    def turn(j, carry):
        for i in range(0, values, SUB):
            inv_t[j, pl.ds(i, SUB), :] = inverse_ref[pl.ds(i * values + j, SUB, stride=values), :]
        return carry

    lax.fori_loop(0, values, turn, 0, unroll=8)

    expected = tm - 1 + (p > 0).astype(jnp.int32) + (p < ns - 1).astype(jnp.int32)
    pl.semaphore_wait(barrier, expected)

    def when_scanner(place, run):
        if scanners == tm:
            run()
        else:
            pl.when(place < scanners)(run)

    def to_scanner(src, dst, d, send, recv):
        place = lax.rem(k + d, tm)
        return pltpu.make_async_remote_copy(
            src_ref=src.at[pl.ds(pl.multiple_of(lax.rem(place, scanners) * rows, SUB), rows)],
            dst_ref=dst.at[k], send_sem=send.at[d], recv_sem=recv.at[d],
            device_id=(place, p), device_id_type=MESH,
        )

    def from_scanner(d):
        place = lax.rem(k + d, tm)
        return pltpu.make_async_remote_copy(
            src_ref=cbuf.at[place],
            dst_ref=cin.at[pl.ds(pl.multiple_of(lax.rem(k, scanners) * rows, SUB), rows)],
            send_sem=c_send.at[d], recv_sem=c_recv.at[d],
            device_id=(place, p), device_id_type=MESH,
        )

    far_first = sorted(range(1, tm), key=lambda d: -min(d, tm - d))
    my_rows = pl.ds(pl.multiple_of(lax.rem(k, scanners) * rows, SUB), rows)
    gains = gain_ref.at[0]
    for d in range(1, tm):
        when_scanner(lax.rem(k + d, tm), lambda d=d: to_scanner(gains, gbuf, d, g_send, g_recv).start())

    def apply_inverse(vector, table=inv_t):
        r_ref[...] = vector
        sums = [None, None]
        for j in range(values):
            term = table[j] * r_ref[j : j + 1, :]
            sums[j % 2] = term if sums[j % 2] is None else sums[j % 2] + term
        return sums[0] + sums[1]

    def up_copy(s):
        return pltpu.make_async_remote_copy(
            src_ref=send_up.at[s], dst_ref=below.at[s], send_sem=up_send.at[s],
            recv_sem=up_recv.at[s], device_id=(k, p + 1), device_id_type=MESH,
        )

    def dn_copy(s):
        return pltpu.make_async_remote_copy(
            src_ref=send_dn.at[s], dst_ref=above.at[s], send_sem=dn_send.at[s],
            recv_sem=dn_recv.at[s], device_id=(k, p - 1), device_id_type=MESH,
        )

    chunks = SWEEPS * steps
    chunk = half // (2 * chunks)
    core = lax.rem(k, 2)
    partner = k + 1 - 2 * core

    def part_of(c):
        return pl.ds(core * (half // 2) + c * chunk, chunk)

    def hand_on(blocks, send, recv, c):
        part = part_of(c)
        return pltpu.make_async_remote_copy(
            src_ref=blocks.at[part], dst_ref=blocks.at[part], send_sem=send.at[c],
            recv_sem=recv.at[c], device_id=(partner, p), device_id_type=MESH,
        )

    def up_blocks_copy(c):
        part = part_of(c)
        return pltpu.make_async_remote_copy(
            src_ref=up_blocks.at[part], dst_ref=below_blocks.at[part], send_sem=ub_send.at[c],
            recv_sem=ub_recv.at[c], device_id=(k, p + 1), device_id_type=MESH,
        )

    def dn_blocks_copy(c):
        part = part_of(c)
        return pltpu.make_async_remote_copy(
            src_ref=dn_blocks.at[part], dst_ref=above_blocks.at[part], send_sem=db_send.at[c],
            recv_sem=db_recv.at[c], device_id=(k, p - 1), device_id_type=MESH,
        )

    def packed(block, index):
        halves = [pick(block[:half], index), pick(block[half:], index)]
        return jnp.concatenate(
            [
                jnp.where(first_half, halves[0][r : r + SUB], halves[1][r : r + SUB])
                for r in range(0, half, SUB)
            ],
            axis=0,
        )

    def unpacked(block, index, mask):
        return masked(
            jnp.concatenate([pick(block, index), pick(block, index + layer)], axis=0), mask
        )

    def sent_halo(s, also):
        @pl.when((p < ns - 1) & also)
        def _():
            up_copy(s).wait_send()

        @pl.when((p > 0) & also)
        def _():
            dn_copy(s).wait_send()

    def split(x):
        high = x.astype(jnp.bfloat16)
        low = (x - high.astype(jnp.float32)).astype(jnp.bfloat16)
        return jnp.concatenate([high, high, low], axis=0)

    def z_faces(stack):
        product = jnp.dot(f_ref[: 2 * values, :], stack, preferred_element_type=jnp.float32)
        return product[:values], product[values:]

    def send_halo(minus_z, plus_z, s):
        send_up[s] = packed(minus_z, high_index)
        send_dn[s] = packed(plus_z, low_index)

        @pl.when(p < ns - 1)
        def _():
            up_copy(s).start()

        @pl.when(p > 0)
        def _():
            dn_copy(s).start()

    def own_part(b, stack, minus_z, plus_z):
        along_xy = jnp.dot(f_ref[2 * values :, :], stack, preferred_element_type=jnp.float32)
        rest = b - masked(pick(minus_z, own_index[4]), own_mask[4])
        rest = rest - masked(pick(plus_z, own_index[5]), own_mask[5])
        for f in range(4):
            product = along_xy[f * values : (f + 1) * values]
            rest = rest - masked(pick(product, own_index[f]), own_mask[f])
        return rest

    def halo(s):
        @pl.when(p < ns - 1)
        def _():
            dn_copy(s).wait_recv()

        @pl.when(p > 0)
        def _():
            up_copy(s).wait_recv()

        return unpacked(below[s], halo_index[0], halo_mask[0]) + unpacked(
            above[s], halo_index[1], halo_mask[1]
        )

    def send_blocks(c):
        def one(n, carry):
            j = core * (half // 2) + c * chunk + n
            first, second = inv_t[j], inv_t[j + half]
            for dst, index in ((up_blocks, high_index), (dn_blocks, low_index)):
                for r in range(0, values, SUB):
                    dst[j, r : r + SUB, :] = jnp.where(
                        first_half, pick(first[r : r + SUB], index), pick(second[r : r + SUB], index)
                    )
            return carry

        lax.fori_loop(0, chunk, one, 0, unroll=True)

        @pl.when(p < ns - 1)
        def _():
            up_blocks_copy(c).start()

        @pl.when(p > 0)
        def _():
            dn_blocks_copy(c).start()

    def share_blocks(c, also):
        @pl.when((p < ns - 1) & also)
        def _():
            dn_blocks_copy(c).wait_recv()
            hand_on(above_blocks, fd_send, fd_recv, c).start()

        @pl.when((p > 0) & also)
        def _():
            up_blocks_copy(c).wait_recv()
            hand_on(below_blocks, fu_send, fu_recv, c).start()

    def take_blocks():
        for c in range(chunks):

            @pl.when(p < ns - 1)
            def _(c=c):
                up_blocks_copy(c).wait_send()
                hand_on(above_blocks, fd_send, fd_recv, c).wait()

            @pl.when(p > 0)
            def _(c=c):
                dn_blocks_copy(c).wait_send()
                hand_on(below_blocks, fu_send, fu_recv, c).wait()

        def one(j, carry):
            under, over = below_blocks[j], above_blocks[j]
            for at in (0, 1):
                for r in range(0, values, SUB):
                    rows_of = slice(r, r + SUB)
                    over_part = jnp.where(
                        halo_mask[1], pick(over[rows_of], halo_index[1] + at * layer), 0.0
                    )
                    halo_inv_t[j + at * half, rows_of, :] = jnp.where(
                        halo_mask[0], pick(under[rows_of], halo_index[0] + at * layer), over_part
                    )
            return carry

        lax.fori_loop(0, half, one, 0, unroll=8)

    def fine_step(m, field):
        b = field + forcing_ref[m]
        x = apply_inverse(b)
        for sweep in range(SWEEPS):
            stack = split(x)
            minus_z, plus_z = z_faces(stack)
            send_halo(minus_z, plus_z, sweep)
            send_blocks(m * SWEEPS + sweep)
            rest = own_part(b, stack, minus_z, plus_z)
            before = m * SWEEPS + sweep - 1
            share_blocks(jnp.maximum(before, 0), before >= 0)
            rest = rest - halo(sweep)
            if sweep == 0:
                sent_halo(SWEEPS - 1, m > 0)
            else:
                sent_halo(sweep - 1, True)
            x = apply_inverse(rest)
        return x

    def both_sweeps(m, field):
        base = 2 * lax.rem(m + 1, 2)
        b = field + forcing_ref[m]
        x = apply_inverse(b)
        stack = split(x)
        minus_z, plus_z = z_faces(stack)
        send_halo(minus_z, plus_z, base)
        inner = apply_inverse(own_part(b, stack, minus_z, plus_z))
        inner_minus, inner_plus = z_faces(split(inner))
        send_halo(inner_minus, inner_plus, base + 1)
        back = jnp.concatenate(
            [
                jnp.where(halo_mask[0], plus_z[r : r + SUB], minus_z[r : r + SUB])
                for r in range(0, values, SUB)
            ],
            axis=0,
        )
        back_minus, back_plus = z_faces(split(apply_inverse(back, halo_inv_t)))
        back = masked(back_minus, halo_mask[0]) + masked(back_plus, halo_mask[1])
        x = inner - apply_inverse(halo(base))
        stack = split(x)
        minus_z, plus_z = z_faces(stack)
        rest = own_part(b, stack, minus_z, plus_z) + back
        x = apply_inverse(rest - halo(base + 1))
        sent_halo(base, True)
        sent_halo(base + 1, True)
        return x

    def carried_in(first):
        for d in far_first:
            when_scanner(
                lax.rem(k + d, tm), lambda d=d: to_scanner(res, rbuf, d, a_send, a_recv).start()
            )

        if first:
            share_blocks(chunks - 1, True)

        def scan():
            rbuf[k] = res[my_rows, :]
            if first:
                gbuf[k] = gains[my_rows, :]
                for d in range(1, tm):
                    to_scanner(gains, gbuf, d, g_send, g_recv).wait_recv()
            for d in range(1, tm):
                to_scanner(res, rbuf, d, a_send, a_recv).wait_recv()
            running = jnp.zeros((rows, LANES), jnp.float32)
            for lap in range(tm):
                cbuf[lap] = running
                running = gbuf[lap] * running + rbuf[lap]
            for d in far_first:
                from_scanner(d).start()
            cin[my_rows, :] = cbuf[k]

        when_scanner(k, scan)
        if first:
            take_blocks()
        for d in range(1, tm):

            def sent(d=d):
                if first:
                    to_scanner(gains, gbuf, d, g_send, g_recv).wait_send()
                to_scanner(res, rbuf, d, a_send, a_recv).wait_send()

            when_scanner(lax.rem(k + d, tm), sent)
            when_scanner(lax.rem(k + tm - d, tm), lambda d=d: from_scanner(d).wait_recv())

        def returned():
            for d in range(1, tm):
                from_scanner(d).wait_send()

        when_scanner(k, returned)
        return cin[...]

    coarse = jnp.zeros((values, elems), jnp.float32)
    previous = coarse
    for iteration in range(ITERS):
        field = lax.fori_loop(
            0, steps, fine_step if iteration == 0 else both_sweeps, jnp.where(k == 0, init_ref[...], previous)
        )
        if iteration == 0:
            sent_halo(SWEEPS - 1, True)
        residual = field - coarse
        res[...] = residual
        carried = carried_in(iteration == 0)
        previous = previous + carried
        coarse = coarse + (gain_ref[0] * carried + residual)
    out_ref[0] = coarse
    out_ref[1] = residual


def body(tm, ns, initial_state, forcing, coarse_gain, block_inverse, face_blocks, neighbor, send_rows):
    values, elems = initial_state.shape
    steps = forcing.shape[0]
    scanners = min(tm, values // SUB)
    rows = values // scanners
    chunks = SWEEPS * steps
    f32 = jnp.float32
    out = jax.ShapeDtypeStruct((2, values, elems), f32)
    vmem = pl.BlockSpec(memory_space=pltpu.VMEM)
    dma = pltpu.SemaphoreType.DMA
    both = (
        pl.pallas_call(
            functools.partial(kernel, tm, ns, steps),
            out_shape=out,
            in_specs=[pl.BlockSpec(memory_space=pl.ANY)] * 7,
            out_specs=vmem,
            scratch_shapes=[
                pltpu.VMEM((values, elems), f32),
                pltpu.VMEM(forcing.shape, f32),
                pltpu.VMEM((1, values, elems), f32),
                pltpu.VMEM((values * values, elems), f32),
                pltpu.VMEM(face_blocks.shape, f32),
                pltpu.VMEM(neighbor.shape, jnp.int32),
                pltpu.VMEM(send_rows.shape, jnp.int32),
                dma((7,)),
                pltpu.VMEM((values, elems), f32),
                pltpu.VMEM((values, values, elems), f32),
                pltpu.VMEM((values, values, elems), f32),
                pltpu.VMEM((6 * values, 3 * values), f32),
                pltpu.VMEM((6 * values, 3 * values), jnp.bfloat16),
                pltpu.VMEM((values, elems), f32),
                pltpu.VMEM((SUB, elems), jnp.int32),
                pltpu.VMEM((values // 2, values, elems), f32),
                pltpu.VMEM((values // 2, values, elems), f32),
                pltpu.VMEM((values // 2, values, elems), f32),
                pltpu.VMEM((values // 2, values, elems), f32),
                pltpu.VMEM((4, values // 2, elems), f32),
                pltpu.VMEM((4, values // 2, elems), f32),
                pltpu.VMEM((4, values // 2, elems), f32),
                pltpu.VMEM((4, values // 2, elems), f32),
                pltpu.VMEM((tm, rows, elems), f32),
                pltpu.VMEM((tm, rows, elems), f32),
                pltpu.VMEM((tm, rows, elems), f32),
                pltpu.VMEM((values, elems), f32),
                dma((4,)), dma((4,)), dma((4,)), dma((4,)),
                dma((chunks,)), dma((chunks,)), dma((chunks,)), dma((chunks,)),
                dma((chunks,)), dma((chunks,)), dma((chunks,)), dma((chunks,)),
                dma((tm,)), dma((tm,)), dma((tm,)), dma((tm,)), dma((tm,)), dma((tm,)),
            ],
            compiler_params=pltpu.CompilerParams(
                collective_id=0, has_side_effects=True, vmem_limit_bytes=63 * 1024 * 1024
            ),
        )(
            initial_state, forcing, coarse_gain,
            block_inverse.reshape(values * values, elems), face_blocks, neighbor, send_rows,
        )
    )
    return both[:1], both[1:]


def solution(mesh):
    return jax.shard_map(
        functools.partial(body, mesh.shape["tm"], mesh.shape["space"]),
        mesh=mesh,
        in_specs=(
            P(None, "space"),
            P("tm", None, "space"),
            P("tm", None, "space"),
            P(None, None, "space"),
            P(),
            P(None, "space"),
            P(None, "space"),
        ),
        out_specs=(P("tm", None, "space"), P("tm", None, "space")),
        check_vma=False,
    )
```
